32 devices in a mesh: groups: 2 (over x), seg: 4 (over z), blk: 4 (over y, core).
Axes of the slice: x: 2, y: 2, z: 4, core: 2. Of those that a mesh axis runs over, the one named last changes fastest.
Arguments:
- base_state: float32 [16, 20, 32, 128], P(('groups', 'seg'), None, 'blk'), parts along dimension 0, may hold values from -6 to 6
- direction: float32 [16, 20, 32, 128], P(('groups', 'seg'), None, 'blk'), parts along dimension 0, may hold values from -6 to 6
- coupling: float32 [40, 20], P('groups'), parts along dimension 0, may hold values from -1.25 to 1.25
- tiles: bfloat16 [8, 32, 16, 128, 128], P('seg', 'blk'), may hold values from -0.15625 to 0.15625
- columns: int32 [8, 32, 16], P('seg', 'blk'), may hold values from 0 to 31, as said below
- wet: int32 [32, 128], P('blk'), may hold values 0 or 1
- basis: float32 [8, 16, 20, 32, 128], P(None, ('groups', 'seg'), None, 'blk'), parts along dimension 1, may hold values from -0.0078125 to 0.0078125
Outputs:
- orthogonal: float32 [16, 20, 32, 128], P(('groups', 'seg'), None, 'blk'), parts along dimension 0
- coefficients: float32 [18], P('groups'), parts along dimension 0
The draws below stay inside these ranges and needn't reach their ends.
There are 2 independent parts, one for each index of `groups`. The reference program is written for one: setup_inputs(seed, part) draws one part's arguments, and reference() takes and returns one part's arrays. A program takes and returns all parts, laid end to end along the dimension named above; an argument that names none is the same for every part. Nothing has to cross between parts.
Inputs may be any that keep to these rules, and one draw needn't show every extreme that they name: columns[s, r, k] = (r + d) mod 32 for some whole d with -2 <= d <= 2; in every segment some entry has d = 2 and some has d = -2.
All inputs are finite; a program needn't handle non-finite values. No bound on the sum of `wet` on one device may be relied on, other than what follows from the above.
Results may differ from the reference program's by a relative error of at most 0.04.
Values may be sent and summed in bfloat16 or wider, within the bound.
A program may use at most 128 MiB of HBM per device.

```python
import jax
import jax.numpy as jnp
from jax import lax

TR = 20
P_SIZE = 128
K = 16
STEPS = 18
KRY = 8
REACH = 2
SEGMENTS = 8
NB = 32


def draw_columns(key, part):
    offsets = jax.random.randint(jax.random.fold_in(key, 11), (SEGMENTS, NB, K), -REACH, REACH + 1)
    offsets = offsets.astype(jnp.int32)
    offsets = offsets.at[:, 0, 0].set(-REACH)
    offsets = offsets.at[:, 1, 0].set(REACH)
    rows = jnp.arange(NB, dtype=jnp.int32)[None, :, None]
    return ((rows + offsets) % NB).astype(jnp.int32)


def set_ends(result, rng, low, top_value):
    extent = result.shape
    spot = [jax.random.randint(jax.random.fold_in(rng, axis), (), 0, extent[axis]) for axis in range(len(extent))]
    result = result.at[tuple(spot)].set(low)
    longest = extent.index(max(extent))
    spot[longest] = (spot[longest] + 1) % extent[longest]
    return result.at[tuple(spot)].set(top_value)


def shard_levels(key, dims, cuts, low, top_value):
    gain = 1.0
    for dim, shards_of in cuts:
        heights = jax.random.uniform(jax.random.fold_in(jax.random.fold_in(key, 6), dim), (shards_of,), jnp.float32, low / len(cuts), top_value / len(cuts))
        gain = gain * jnp.repeat(jnp.exp(heights), dims[dim] // shards_of).reshape((-1,) + (1,) * (len(dims) - 1 - dim))
    return gain


def noise(rng, shape, spread, most, cuts=(), kind=jnp.bfloat16):
    result = jax.random.normal(rng, shape, jnp.float32) * spread
    if len(cuts) > 0:
        result = shard_levels(rng, shape, cuts, -0.22, 0.18) * result
    return jnp.clip(result, min=-most, max=most).astype(kind)


def setup_inputs(seed: int = 0, part: int = 0) -> dict:
    arg_keys = jax.random.split(jax.random.key(seed), 8)
    part_keys = jax.random.split(jax.random.fold_in(arg_keys[7], part), 8)
    base_state = noise(part_keys[0], (SEGMENTS, TR, NB, P_SIZE), 1.0, 6.0, ((0, 4), (2, 4)), jnp.float32)
    direction = noise(part_keys[1], (SEGMENTS, TR, NB, P_SIZE), 1.0, 6.0, ((0, 4), (2, 4)), jnp.float32)
    coupling = noise(part_keys[2], (TR, TR), TR ** -0.5, 1.25, (), jnp.float32)
    tiles = noise(arg_keys[3], (SEGMENTS, NB, K, P_SIZE, P_SIZE), (K * P_SIZE * 5 // 6) ** -0.5, 0.15625, ((0, 4), (1, 4)))
    columns = draw_columns(jax.random.fold_in(arg_keys[7], 71), part)
    wet = set_ends((jax.random.randint(arg_keys[5], (NB, P_SIZE), 0, 4) < 3).astype(jnp.int32), jax.random.fold_in(arg_keys[5], 1), 0, 1)
    basis = noise(part_keys[6], (KRY, SEGMENTS, TR, NB, P_SIZE), (SEGMENTS * TR * NB * P_SIZE) ** -0.5, 0.0078125, ((1, 4), (3, 4)), jnp.float32)
    return {"base_state": base_state, "direction": direction, "coupling": coupling, "tiles": tiles, "columns": columns, "wet": wet, "basis": basis}


def one_segment(items, coupling, wetf):
    state, start, tiles_s, cols_s = items
    slope = 1.0 - jnp.tanh(state) ** 2
    flat = cols_s.reshape(-1).astype(jnp.int32)
    tiles_f = tiles_s.astype(jnp.float32)

    def advance(u, unused):
        source = jnp.einsum('tu,unp->tnp', coupling, slope * u, precision=lax.Precision.HIGHEST)
        drive = (u + 0.5 * source).astype(jnp.bfloat16)
        picked = jnp.take(drive, flat, axis=1).reshape(TR, NB, K, P_SIZE)
        moved = jnp.einsum('rkpq,trkq->trp', tiles_f, picked.astype(jnp.float32))
        return (moved * wetf, None)
    final, unused = lax.scan(advance, start, None, length=STEPS)
    return final

def reference(base_state, direction, coupling, tiles, columns, wet, basis):
    wetf = wet.astype(jnp.float32)
    finals = lax.map(lambda items: one_segment(items, coupling, wetf), (base_state, direction, tiles, columns))
    shot = finals - jnp.roll(direction, -1, axis=0)
    proj = jnp.einsum('jstnp,stnp->j', basis, shot, precision=lax.Precision.HIGHEST)
    orthogonal = shot - jnp.einsum('j,jstnp->stnp', proj, basis, precision=lax.Precision.HIGHEST)
    entries = float(SEGMENTS * TR * NB * P_SIZE)
    length = jnp.sqrt(jnp.sum(orthogonal * orthogonal) / entries)
    return (orthogonal, jnp.concatenate([proj, length[None]]))
```

```python
import functools

import jax
import jax.numpy as jnp
from jax import lax
from jax.experimental import pallas as pl
from jax.experimental.pallas import tpu as pltpu
from jax.sharding import PartitionSpec as P

STEPS = 18
MESH = pl.DeviceIdType.MESH
REACH = 2
PAD = 32
BATCH = 4


def merge_kernel(total, rows, stored, cols_ref, tiles_ref, wet_ref, w_ref, acc0, acc1):
    s, g = pl.program_id(0), pl.program_id(1)
    first = lax.axis_index("blk") * rows
    wide = 2 * REACH + 1
    accs = (acc0, acc1)
    for acc in accs:
        acc[...] = jnp.zeros_like(acc)

    def add(k, unused):
        for j in range(2):
            row = 2 * g + j
            col = cols_ref[s, row, k]
            d = lax.rem(col - first - row + (REACH + total), total)
            accs[j][d] += tiles_ref[0, j, k].astype(jnp.float32)
        return unused

    lax.fori_loop(0, stored, add, 0, unroll=4)
    size = acc0.shape[1]
    for j in range(2):
        wet = wet_ref[pl.ds(2 * g + j, 1), :].astype(jnp.float32)
        for c in range(wide + 1):
            d = c - j
            if 0 <= d < wide:
                part = (accs[j][d].T * wet).astype(jnp.bfloat16)
            else:
                part = jnp.zeros((size, size), jnp.bfloat16)
            w_ref[0, 0, c * size:(c + 1) * size, j * size:(j + 1) * size] = part


def steps_kernel(
    dims, base_ref, dir_ref, coup_ref, w, basis, orth_ref, coef_ref,
    drive0, drive1, slope, cc, follow, whalo, shalo, sent, came, part1, part2, gram1, gram2,
    init_send, init_recv, send_sem, recv_sem, follow_sem, red_sem1, red_sem2, gram_sem1, gram_sem2,
):
    segs, tracers, rows, points, kry, n_seg, n_blk, entries = dims
    pairs = rows // 2
    per = tracers * rows
    pair = 2 * points
    drive = (drive0, drive1)
    me_seg, me_blk = lax.axis_index("seg"), lax.axis_index("blk")
    left, right = lax.rem(me_blk + n_blk - 1, n_blk), lax.rem(me_blk + 1, n_blk)

    barrier = pltpu.get_barrier_semaphore()
    for i in range(1, n_blk):
        pl.semaphore_signal(barrier, inc=1, device_id={"blk": lax.rem(me_blk + i, n_blk)}, device_id_type=MESH)
    for i in range(1, n_seg):
        pl.semaphore_signal(barrier, inc=1, device_id={"seg": lax.rem(me_seg + i, n_seg)}, device_id_type=MESH)

    def lanes_of(g, count=1):
        return slice((g + 1) * pair, (g + 1 + count) * pair)

    def dot(a, b):
        return jnp.dot(a, b, preferred_element_type=jnp.float32)

    c = 0.5 * coup_ref[...]
    high = c.astype(jnp.bfloat16)
    low = (c - high.astype(jnp.float32)).astype(jnp.bfloat16)
    cc[...] = jnp.zeros_like(cc)
    cc[:tracers, 0:tracers] = high.astype(jnp.float32)
    cc[:tracers, PAD:PAD + tracers] = low.astype(jnp.float32)
    one = cc[...]
    blank = jnp.zeros_like(one)
    mix = jnp.concatenate(
        [
            jnp.concatenate([one if i == j else blank for j in range(BATCH)], axis=1)
            for i in range(BATCH)
        ],
        axis=0,
    ).astype(jnp.bfloat16)
    slope[...] = jnp.zeros_like(slope)
    for r in range(rows):
        lanes = slice(r * points, (r + 1) * points)
        for s in range(segs):
            t = jnp.tanh(base_ref[pl.ds(s * per + r, tracers, stride=rows), :])
            slope[s, :tracers, lanes] = 1.0 - t * t

    def force(us, ks):
        out = []
        for i in range(0, len(us), BATCH):
            group = us[i:i + BATCH]
            n = len(group)
            xs = [(k * u).astype(jnp.bfloat16) for u, k in zip(group, ks[i:i + BATCH])]
            stack = jnp.concatenate([x for x in xs for unused in range(2)], axis=0)
            added = dot(mix[:n * PAD, :2 * n * PAD], stack)
            out += [(u + added[j * PAD:(j + 1) * PAD]).astype(jnp.bfloat16) for j, u in enumerate(group)]
        return out

    def force_into(units, to):
        values = force([u for u, k, s, g in units], [k for u, k, s, g in units])
        for (u, k, s, g), v in zip(units, values):
            to[s, :, lanes_of(g)] = v

    def slope_of(s, g):
        return slope[s, :, g * pair:(g + 1) * pair]

    def start_of(s, g):
        halves = [
            jnp.concatenate(
                [
                    dir_ref[pl.ds(s * per + 2 * g + j, tracers, stride=rows), :],
                    jnp.zeros((PAD - tracers, points), jnp.float32),
                ],
                axis=0,
            )
            for j in range(2)
        ]
        return jnp.concatenate(halves, axis=1)

    edges = (0, pairs - 1)
    halo = (-1, pairs)

    def initial(i, src, dst, side):
        return pltpu.make_async_remote_copy(
            src_ref=src, dst_ref=dst, send_sem=init_send.at[i], recv_sem=init_recv.at[i],
            device_id={"blk": (left, right)[side]}, device_id_type=MESH,
        )

    first = [
        initial(
            2 * s + side, drive0.at[s, :, lanes_of(edges[side])], drive0.at[s, :, lanes_of(halo[1 - side])], side
        )
        for s in range(segs)
        for side in range(2)
    ]
    slopes = [
        initial(
            2 * segs + 2 * s + side, slope.at[s, :, edges[side] * pair:(edges[side] + 1) * pair],
            shalo.at[1 - side, s], side,
        )
        for s in range(segs)
        for side in range(2)
    ]
    borders = [
        initial(
            4 * segs + 2 * s + side, w.at[s, edges[side], (side * 2) * pair:(side * 2 + 1) * pair, :],
            whalo.at[1 - side, s], side,
        )
        for s in range(segs)
        for side in range(2)
    ]
    force_into([(start_of(s, g), slope_of(s, g), s, g) for s in range(segs) for g in edges], drive0)
    pl.semaphore_wait(barrier, n_blk + n_seg - 2)
    for x in first + slopes + borders:
        x.start()
    follow_copy = pltpu.make_async_remote_copy(
        src_ref=dir_ref.at[0:per], dst_ref=follow, send_sem=follow_sem.at[0], recv_sem=follow_sem.at[1],
        device_id={"seg": lax.rem(me_seg + n_seg - 1, n_seg)}, device_id_type=MESH,
    )
    follow_copy.start()
    inner = range(1, pairs - 1)
    force_into([(start_of(s, g), slope_of(s, g), s, g) for s in range(segs) for g in inner], drive0)

    chunks = segs * tracers
    half = kry // 2 + 1

    def fold(a):
        return jnp.sum(a, axis=0, keepdims=True)

    def everyone(part, me, axis, count, sems):
        return [
            pltpu.make_async_remote_copy(
                src_ref=part.at[me], dst_ref=part.at[me],
                send_sem=sems.at[0, i - 1], recv_sem=sems.at[1, i - 1],
                device_id={axis: lax.rem(me + i, count)}, device_id_type=MESH,
            )
            for i in range(1, count)
        ]

    def total_of(part, copies, count):
        for x in copies:
            x.wait()
        result = part[0]
        for i in range(1, count):
            result = result + part[i]
        return result

    def gram(i, acc):
        b = [basis[j, pl.ds(pl.multiple_of(i * rows, rows), rows), :] for j in range(kry)]
        return tuple(acc[m * kry + j] + b[j] * b[(j + m) % kry] for m in range(half) for j in range(kry))

    zero = jnp.zeros((rows, points), jnp.float32)
    sums = lax.fori_loop(0, chunks, gram, (zero,) * (half * kry))
    for m in range(half):
        for j in range(kry):
            gram1[me_blk, pl.ds(m * 8 + j, 1), :] = fold(sums[m * kry + j])
    gram_copies1 = everyone(gram1, me_blk, "blk", n_blk, gram_sem1)
    for x in gram_copies1:
        x.start()

    def message(n, side):
        return pltpu.make_async_remote_copy(
            src_ref=sent.at[n, side], dst_ref=came.at[n, 1 - side],
            send_sem=send_sem.at[n, side], recv_sem=recv_sem.at[n, 1 - side],
            device_id={"blk": (left, right)[side]}, device_id_type=MESH,
        )

    def arrival(n, side):
        return pltpu.make_async_remote_copy(
            src_ref=sent.at[n, 1 - side], dst_ref=came.at[n, side],
            send_sem=send_sem.at[n, 1 - side], recv_sem=recv_sem.at[n, side],
            device_id={"blk": (left, right)[1 - side]}, device_id_type=MESH,
        )

    def step(n, slot, halos, finish):
        here, there = drive[slot], drive[1 - slot]
        own = [[None, None] for s in range(segs)]
        for s in range(segs):
            own[s][0] = dot(here[s, :, lanes_of(0, 2)], w[s, 0, pair:3 * pair, :])
            own[s][1] = dot(here[s, :, lanes_of(pairs - 2, 2)], w[s, pairs - 1, 0:2 * pair, :])
        if not finish:
            for side in range(2):
                for s in range(segs):
                    sent[n, side, s] = own[s][side].astype(jnp.bfloat16)
            for side in range(2):
                message(n, side).start()
        moved = {}
        for s in range(segs):
            for g in range(1, pairs - 1):
                moved[s, g] = dot(here[s, :, lanes_of(g - 1, 3)], w[s, g])
        if halos:
            mine = [
                [dot(there[s, :, lanes_of(edges[side])], whalo[side, s]) for side in range(2)] for s in range(segs)
            ]
        if not finish:
            force_into([(moved[s, g], slope_of(s, g), s, g) for s in range(segs) for g in inner], there)
        if halos:
            for side in range(2):
                arrival(n - 1, side).wait()
            force_into(
                [
                    (mine[s][side] + came[n - 1, side, s].astype(jnp.float32), shalo[side, s], s, halo[side])
                    for s in range(segs)
                    for side in range(2)
                ],
                here,
            )
        else:
            for x in first:
                x.wait()
        for side in range(2):
            g = edges[side]
            for s in range(segs):
                moved[s, g] = own[s][side] + dot(
                    here[s, :, lanes_of(halo[side])], w[s, g, side * 2 * pair:(side * 2 + 1) * pair, :]
                )
        if finish:
            for s in range(segs):
                for g in range(pairs):
                    for j in range(2):
                        orth_ref[pl.ds(s * per + 2 * g + j, tracers, stride=rows), :] = (
                            moved[s, g][:tracers, j * points:(j + 1) * points]
                        )
        else:
            force_into([(moved[s, g], slope_of(s, g), s, g) for s in range(segs) for g in edges], there)

    step(0, 0, False, False)
    for x in slopes + borders:
        x.wait()

    def two(i, unused):
        step(2 * i + 1, 1, True, False)
        step(2 * i + 2, 0, True, False)
        return unused

    lax.fori_loop(0, (STEPS - 2) // 2, two, 0)
    step(STEPS - 1, 1, True, True)

    gram2[me_seg] = total_of(gram1, gram_copies1, n_blk)
    gram_copies2 = everyone(gram2, me_seg, "seg", n_seg, gram_sem2)
    for x in gram_copies2:
        x.start()
    follow_copy.wait()

    def project(i, acc):
        here = pl.ds(pl.multiple_of(i * rows, rows), rows)
        for s in range(segs):
            at = pl.ds(pl.multiple_of(i * rows, rows) + s * per, rows)
            if s < segs - 1:
                nxt = dir_ref[pl.ds(pl.multiple_of(i * rows, rows) + (s + 1) * per, rows), :]
            else:
                nxt = follow[here, :]
            shot = orth_ref[at, :] - nxt
            orth_ref[at, :] = shot
            acc = tuple(acc[j] + basis[j, at, :] * shot for j in range(kry)) + (acc[kry] + shot * shot,)
        return acc

    sums = lax.fori_loop(0, tracers, project, (zero,) * (kry + 1), unroll=4)
    for j in range(kry):
        part1[me_blk, pl.ds(j, 1), :] = fold(sums[j])
    part1[me_blk, pl.ds(8, 8), :] = sums[kry]

    copies = everyone(part1, me_blk, "blk", n_blk, red_sem1)
    for x in copies:
        x.start()
    part2[me_seg] = total_of(part1, copies, n_blk)
    copies = everyone(part2, me_seg, "seg", n_seg, red_sem2)
    for x in copies:
        x.start()
    gramd = jnp.sum(total_of(gram2, gram_copies2, n_seg), axis=1, keepdims=True)
    sumd = jnp.sum(total_of(part2, copies, n_seg), axis=1, keepdims=True)
    h = sumd[0:kry]
    hv = [sumd[j:j + 1] for j in range(kry)]
    quad = jnp.zeros((kry, 1), jnp.float32)
    for m in range(half):
        turned = h if m == 0 else jnp.concatenate([h[m:], h[:m]], axis=0)
        weight = 1.0 if m == 0 or 2 * m == kry else 2.0
        quad = quad + weight * (turned * gramd[m * 8:m * 8 + kry])
    quad = h * (quad - 2.0 * h) + sumd[8:16]
    square = jnp.sum(jnp.broadcast_to(quad, (kry, points)), axis=0, keepdims=True)
    length = jnp.sqrt(jnp.maximum(square, 0.0) / entries)
    coef_ref[kry] = length[0, 0]
    for j in range(kry):
        coef_ref[j] = hv[j][0, 0]
    wide = [jnp.broadcast_to(x, (rows, points)) for x in hv]

    def subtract(i, unused):
        at = pl.ds(pl.multiple_of(i * rows, rows), rows)
        a = hv_sum([wide[j] * basis[j, at, :] for j in range(kry)])
        orth_ref[at, :] = orth_ref[at, :] - a
        return unused

    lax.fori_loop(0, chunks, subtract, 0, unroll=4)


def hv_sum(terms):
    while len(terms) > 1:
        terms = [sum(terms[i:i + 2]) for i in range(0, len(terms), 2)]
    return terms[0]


def on_device(n_seg, n_blk, base_state, direction, coupling, tiles, columns, wet, basis):
    segs, tracers, rows, points = direction.shape
    stored = tiles.shape[2]
    kry = basis.shape[0]
    total = rows * n_blk
    entries = float(segs * n_seg * tracers * total * points)
    pairs = rows // 2
    pair = 2 * points
    wide = 2 * REACH + 2
    w = pl.pallas_call(
        functools.partial(merge_kernel, total, rows, stored),
        out_shape=jax.ShapeDtypeStruct((segs, pairs, wide * points, 2 * points), jnp.bfloat16),
        grid_spec=pltpu.PrefetchScalarGridSpec(
            num_scalar_prefetch=1,
            grid=(segs, pairs),
            in_specs=[
                pl.BlockSpec((1, 2, stored, points, points), lambda s, g, c: (s, g, 0, 0, 0)),
                pl.BlockSpec((rows, points), lambda s, g, c: (0, 0)),
            ],
            out_specs=pl.BlockSpec((1, 1, wide * points, 2 * points), lambda s, g, c: (s, g, 0, 0)),
            scratch_shapes=[pltpu.VMEM((2 * REACH + 1, points, points), jnp.float32)] * 2,
        ),
        compiler_params=pltpu.CompilerParams(vmem_limit_bytes=48 << 20),
        name="merge",
    )(columns, tiles, wet)
    flat = segs * tracers * rows
    dims = (segs, tracers, rows, points, kry, n_seg, n_blk, entries)
    in_vmem = pl.BlockSpec(memory_space=pltpu.VMEM)
    half = (kry // 2 + 1) * 8
    orth, coef = pl.pallas_call(
        functools.partial(steps_kernel, dims),
        out_shape=(
            jax.ShapeDtypeStruct((flat, points), jnp.float32),
            jax.ShapeDtypeStruct((kry + 1,), jnp.float32),
        ),
        in_specs=[in_vmem] * 5,
        out_specs=(in_vmem, pl.BlockSpec(memory_space=pltpu.SMEM)),
        scratch_shapes=[
            pltpu.VMEM((segs, PAD, (pairs + 2) * pair), jnp.bfloat16),
            pltpu.VMEM((segs, PAD, (pairs + 2) * pair), jnp.bfloat16),
            pltpu.VMEM((segs, PAD, rows * points), jnp.float32),
            pltpu.VMEM((PAD, 2 * PAD), jnp.float32),
            pltpu.VMEM((tracers * rows, points), jnp.float32),
            pltpu.VMEM((2, segs, pair, pair), jnp.bfloat16),
            pltpu.VMEM((2, segs, PAD, pair), jnp.float32),
            pltpu.VMEM((STEPS - 1, 2, segs, PAD, pair), jnp.bfloat16),
            pltpu.VMEM((STEPS - 1, 2, segs, PAD, pair), jnp.bfloat16),
            pltpu.VMEM((n_blk, 16, points), jnp.float32),
            pltpu.VMEM((n_seg, 16, points), jnp.float32),
            pltpu.VMEM((n_blk, half, points), jnp.float32),
            pltpu.VMEM((n_seg, half, points), jnp.float32),
            pltpu.SemaphoreType.DMA((6 * segs,)),
            pltpu.SemaphoreType.DMA((6 * segs,)),
            pltpu.SemaphoreType.DMA((STEPS - 1, 2)),
            pltpu.SemaphoreType.DMA((STEPS - 1, 2)),
            pltpu.SemaphoreType.DMA((2,)),
            pltpu.SemaphoreType.DMA((2, n_blk - 1)),
            pltpu.SemaphoreType.DMA((2, n_seg - 1)),
            pltpu.SemaphoreType.DMA((2, n_blk - 1)),
            pltpu.SemaphoreType.DMA((2, n_seg - 1)),
        ],
        compiler_params=pltpu.CompilerParams(
            collective_id=0, has_side_effects=True, vmem_limit_bytes=40 << 20
        ),
        name="steps",
    )(
        base_state.reshape(flat, points), direction.reshape(flat, points), coupling,
        w, basis.reshape(kry, flat, points),
    )
    return orth.reshape(direction.shape), coef


def solution(mesh):
    in_specs = (
        P(("groups", "seg"), None, "blk", None),
        P(("groups", "seg"), None, "blk", None),
        P("groups", None),
        P("seg", "blk", None, None, None),
        P("seg", "blk", None),
        P("blk", None),
        P(None, ("groups", "seg"), None, "blk", None),
    )
    out_specs = (P(("groups", "seg"), None, "blk", None), P("groups"))
    body = functools.partial(on_device, mesh.shape["seg"], mesh.shape["blk"])
    return jax.shard_map(body, mesh=mesh, in_specs=in_specs, out_specs=out_specs, check_vma=False)
```

```python
import functools

import jax
import jax.numpy as jnp
from jax import lax
from jax.experimental import pallas as pl
from jax.experimental.pallas import tpu as pltpu
from jax.sharding import PartitionSpec as P

STEPS = 18
MESH = pl.DeviceIdType.MESH
REACH = 2
PAD = 32
BATCH = 4
BORDER = (((0, 0), (1, 0), (1, 1)), ((0, 0), (0, 1), (1, 1)))


def merge_pair(total, first, stored, row, cols_at, tile_at, wet, accs, put):
    wide = 2 * REACH + 1
    for acc in accs:
        acc[...] = jnp.zeros_like(acc)

    def add(k, unused):
        for j in range(2):
            col = cols_at(row + j, k)
            d = lax.rem(col - first - row - j + (REACH + total), total)
            accs[j][d] += tile_at(j, k).astype(jnp.float32)
        return unused

    lax.fori_loop(0, stored, add, 0, unroll=4)
    size = accs[0].shape[1]
    for j in range(2):
        mask = wet(row + j).astype(jnp.float32)
        for c in range(wide + 1):
            d = c - j
            if 0 <= d < wide:
                put(c, j, (accs[j][d].T * mask).astype(jnp.bfloat16))
            else:
                put(c, j, jnp.zeros((size, size), jnp.bfloat16))


def merge_pairs(total, rows, groups, cols, wet_v, tile_buf, waits, accs, w_ref, then=None):
    first = lax.axis_index("blk") * rows
    segs = cols.shape[0]
    size = accs[0].shape[1]
    for i, g in enumerate(groups):
        for s in range(segs):
            for x in waits[i * segs + s]:
                x.wait()

            def put(c, j, part):
                w_ref[s, i, c * size:(c + 1) * size, j * size:(j + 1) * size] = part

            merge_pair(
                total, first, cols.shape[2], 2 * g, lambda row, k: cols[s, row, k],
                lambda j, k: tile_buf[s, 2 * i + j, k],
                lambda row: wet_v[pl.ds(row, 1), :], accs, put,
            )
            if then is not None:
                then(i, s)


def start_fetches(groups, cols_ref, wet_ref, tiles_ref, cols, wet_v, tile_buf, small_sem, tile_sem):
    small = [
        pltpu.make_async_copy(cols_ref, cols, small_sem.at[0]),
        pltpu.make_async_copy(wet_ref, wet_v, small_sem.at[1]),
    ]
    waits = []
    for i, g in enumerate(groups):
        for s in range(cols_ref.shape[0]):
            waits.append(
                [
                    pltpu.make_async_copy(
                        tiles_ref.at[s, 2 * g + j], tile_buf.at[s, 2 * i + j], tile_sem.at[s, 2 * i + j]
                    )
                    for j in range(2)
                ]
            )
    for x in small:
        x.start()
    for both in waits:
        for x in both:
            x.start()
    return small, waits


def mix_of(coup_ref, cc):
    tracers = coup_ref.shape[0]
    c = 0.5 * coup_ref[...]
    high = c.astype(jnp.bfloat16)
    low = (c - high.astype(jnp.float32)).astype(jnp.bfloat16)
    cc[...] = jnp.zeros_like(cc)
    cc[:tracers, 0:tracers] = high.astype(jnp.float32)
    cc[:tracers, PAD:PAD + tracers] = low.astype(jnp.float32)
    one = cc[...]
    blank = jnp.zeros_like(one)
    return jnp.concatenate(
        [
            jnp.concatenate([one if i == j else blank for j in range(BATCH)], axis=1)
            for i in range(BATCH)
        ],
        axis=0,
    ).astype(jnp.bfloat16)


def dot(a, b):
    return jnp.dot(a, b, preferred_element_type=jnp.float32)


def forced(mix, us, ks):
    out = []
    for i in range(0, len(us), BATCH):
        group = us[i:i + BATCH]
        n = len(group)
        xs = [(k * u).astype(jnp.bfloat16) for u, k in zip(group, ks[i:i + BATCH])]
        stack = jnp.concatenate([x for x in xs for unused in range(2)], axis=0)
        added = dot(mix[:n * PAD, :2 * n * PAD], stack)
        out += [(u + added[j * PAD:(j + 1) * PAD]).astype(jnp.bfloat16) for j, u in enumerate(group)]
    return out


def edge_kernel(
    dims, base_hbm, dir_hbm, coup_hbm, cols_ref, wet_ref, tiles_ref, w_ref, slope_ref, drive_ref, left_ref, right_ref,
    cols, wet_v, tile_buf, acc0, acc1, cc, base, direction, coup, w_v, slope_v, drive_v, out_v,
    small_sem, tile_sem, in_sem, w_sem, out_sem,
):
    segs, tracers, rows, points, total = dims
    pairs = rows // 2
    per = tracers * rows
    pair = 2 * points
    edges = (0, pairs - 1)
    fetches = [
        pltpu.make_async_copy(a, b, in_sem.at[i])
        for i, (a, b) in enumerate([(base_hbm, base), (dir_hbm, direction), (coup_hbm, coup)])
    ]
    for x in fetches:
        x.start()
    small, waits = start_fetches(edges, cols_ref, wet_ref, tiles_ref, cols, wet_v, tile_buf, small_sem, tile_sem)
    for x in fetches:
        x.wait()
    mix = mix_of(coup, cc)

    def native(ref, s, g):
        halves = [
            jnp.concatenate(
                [
                    ref[pl.ds(s * per + 2 * g + j, tracers, stride=rows), :],
                    jnp.zeros((PAD - tracers, points), jnp.float32),
                ],
                axis=0,
            )
            for j in range(2)
        ]
        return jnp.concatenate(halves, axis=1)

    units = [(s, g) for s in range(segs) for g in range(pairs)]
    slopes, starts = [], []
    for s, g in units:
        t = jnp.tanh(native(base, s, g))
        k = 1.0 - t * t
        slope_v[s, :, g * pair:(g + 1) * pair] = k
        slopes.append(k)
        starts.append(native(direction, s, g))
    drives = forced(mix, starts, slopes)
    for (s, g), d, k in zip(units, drives, slopes):
        drive_v[s, :, g * pair:(g + 1) * pair] = d
        if g in edges:
            high = k.astype(jnp.bfloat16)
            low = (k - high.astype(jnp.float32)).astype(jnp.bfloat16)
            for i, x in enumerate((d, high, low)):
                for j in range(2):
                    at = 3 * points + (2 * i + j) * PAD
                    out_v[edges.index(g), s, at:at + PAD, :] = x[:, j * points:(j + 1) * points]
    for x in small:
        x.wait()
    outs = [
        pltpu.make_async_copy(slope_v, slope_ref, out_sem.at[0]),
        pltpu.make_async_copy(drive_v, drive_ref, out_sem.at[1]),
    ]
    for x in outs:
        x.start()

    def merged(i, s):
        for n, (c, j) in enumerate(BORDER[i]):
            c = c + i * 2 * REACH
            out_v[i, s, n * points:(n + 1) * points, :] = (
                w_v[s, i, c * points:(c + 1) * points, j * points:(j + 1) * points]
            )
        copy = pltpu.make_async_copy(w_v.at[s, i], w_ref.at[s, i], w_sem.at[s, i])
        copy.start()
        outs.append(copy)
        if s == segs - 1:
            copy = pltpu.make_async_copy(out_v.at[i], (left_ref, right_ref)[i], out_sem.at[2 + i])
            copy.start()
            outs.append(copy)

    merge_pairs(total, rows, edges, cols, wet_v, tile_buf, waits, (acc0, acc1), w_v, merged)
    for x in outs:
        x.wait()


def inner_kernel(
    dims, basis, cols_ref, wet_ref, tiles_ref, w_ref, gram_ref,
    cols, wet_v, tile_buf, acc0, acc1, small_sem, tile_sem,
):
    segs, tracers, rows, points, total = dims
    pairs = rows // 2
    kry = basis.shape[0]
    groups = tuple(range(1, pairs - 1))
    small, waits = start_fetches(groups, cols_ref, wet_ref, tiles_ref, cols, wet_v, tile_buf, small_sem, tile_sem)
    half = kry // 2 + 1

    def gram(i, acc):
        b = [basis[j, pl.ds(pl.multiple_of(i * rows, rows), rows), :] for j in range(kry)]
        return tuple(acc[m * kry + j] + b[j] * b[(j + m) % kry] for m in range(half) for j in range(kry))

    zero = jnp.zeros((rows, points), jnp.float32)
    sums = lax.fori_loop(0, segs * tracers, gram, (zero,) * (half * kry))
    for m in range(half):
        for j in range(kry):
            gram_ref[pl.ds(m * 8 + j, 1), :] = jnp.sum(sums[m * kry + j], axis=0, keepdims=True)
    for x in small:
        x.wait()
    merge_pairs(total, rows, groups, cols, wet_v, tile_buf, waits, (acc0, acc1), w_ref)


def steps_kernel(
    dims, slope, start, dir_ref, coup_ref, w_edge, w_inner, from_left, from_right, gram_in, basis, orth_ref, coef_ref,
    drive0, drive1, cc, follow, whalo, sent, came, part1, part2, gram1, gram2,
    send_sem, recv_sem, follow_sem, red_sem1, red_sem2, gram_sem1, gram_sem2,
):
    segs, tracers, rows, points, kry, n_seg, n_blk, entries = dims
    pairs = rows // 2
    per = tracers * rows
    pair = 2 * points
    drive = (drive0, drive1)
    me_seg, me_blk = lax.axis_index("seg"), lax.axis_index("blk")
    left, right = lax.rem(me_blk + n_blk - 1, n_blk), lax.rem(me_blk + 1, n_blk)

    barrier = pltpu.get_barrier_semaphore()
    for i in range(1, n_blk):
        pl.semaphore_signal(barrier, inc=1, device_id={"blk": lax.rem(me_blk + i, n_blk)}, device_id_type=MESH)
    for i in range(1, n_seg):
        pl.semaphore_signal(barrier, inc=1, device_id={"seg": lax.rem(me_seg + i, n_seg)}, device_id_type=MESH)

    def lanes_of(g, count=1):
        return slice((g + 1) * pair, (g + 1 + count) * pair)

    mix = mix_of(coup_ref, cc)
    halos_in = (from_left, from_right)

    def force_into(units, to):
        values = forced(mix, [u for u, k, s, g in units], [k for u, k, s, g in units])
        for (u, k, s, g), v in zip(units, values):
            to[s, :, lanes_of(g)] = v

    def slope_of(s, g):
        return slope[s, :, g * pair:(g + 1) * pair]

    def beyond(s, side, i):
        at = 3 * points + 2 * i * PAD
        ref = halos_in[side]
        return jnp.concatenate([ref[s, at:at + PAD, :], ref[s, at + PAD:at + 2 * PAD, :]], axis=1)

    def slope_beyond(s, side):
        return beyond(s, side, 1).astype(jnp.float32) + beyond(s, side, 2).astype(jnp.float32)

    edges = (0, pairs - 1)
    inner = range(1, pairs - 1)
    halo = (-1, pairs)
    for s in range(segs):
        drive0[s, :, pair:(pairs + 1) * pair] = start[s]
        for side in range(2):
            drive0[s, :, lanes_of(halo[side])] = beyond(s, side, 0)
            whalo[side, s] = jnp.zeros((pair, pair), jnp.bfloat16)
            for n, (c, j) in enumerate(BORDER[1 - side]):
                whalo[side, s, c * points:(c + 1) * points, j * points:(j + 1) * points] = (
                    halos_in[side][s, n * points:(n + 1) * points, :]
                )
    gram1[me_blk] = gram_in[...]
    follow_copy = pltpu.make_async_remote_copy(
        src_ref=dir_ref.at[0:per], dst_ref=follow, send_sem=follow_sem.at[0], recv_sem=follow_sem.at[1],
        device_id={"seg": lax.rem(me_seg + n_seg - 1, n_seg)}, device_id_type=MESH,
    )
    chunks = segs * tracers
    half = kry // 2 + 1

    def fold(a):
        return jnp.sum(a, axis=0, keepdims=True)

    def everyone(part, me, axis, count, sems):
        return [
            pltpu.make_async_remote_copy(
                src_ref=part.at[me], dst_ref=part.at[me],
                send_sem=sems.at[0, i - 1], recv_sem=sems.at[1, i - 1],
                device_id={axis: lax.rem(me + i, count)}, device_id_type=MESH,
            )
            for i in range(1, count)
        ]

    def total_of(part, copies, count):
        for x in copies:
            x.wait()
        result = part[0]
        for i in range(1, count):
            result = result + part[i]
        return result

    zero = jnp.zeros((rows, points), jnp.float32)
    gram_copies1 = everyone(gram1, me_blk, "blk", n_blk, gram_sem1)

    def message(n, side):
        return pltpu.make_async_remote_copy(
            src_ref=sent.at[n, side], dst_ref=came.at[n, 1 - side],
            send_sem=send_sem.at[n, side], recv_sem=recv_sem.at[n, 1 - side],
            device_id={"blk": (left, right)[side]}, device_id_type=MESH,
        )

    def arrival(n, side):
        return pltpu.make_async_remote_copy(
            src_ref=sent.at[n, 1 - side], dst_ref=came.at[n, side],
            send_sem=send_sem.at[n, 1 - side], recv_sem=recv_sem.at[n, side],
            device_id={"blk": (left, right)[1 - side]}, device_id_type=MESH,
        )

    def step(n, slot, halos, finish):
        here, there = drive[slot], drive[1 - slot]
        own = [[None, None] for s in range(segs)]
        for s in range(segs):
            own[s][0] = dot(here[s, :, lanes_of(0, 2)], w_edge[s, 0, pair:3 * pair, :])
            own[s][1] = dot(here[s, :, lanes_of(pairs - 2, 2)], w_edge[s, 1, 0:2 * pair, :])
        def send():
            for side in range(2):
                for s in range(segs):
                    sent[n, side, s] = own[s][side].astype(jnp.bfloat16)
            if not halos:
                pl.semaphore_wait(barrier, n_blk + n_seg - 2)
            for side in range(2):
                message(n, side).start()

        if halos and not finish:
            send()
        moved = {}
        for s in range(segs):
            for g in range(1, pairs - 1):
                moved[s, g] = dot(here[s, :, lanes_of(g - 1, 3)], w_inner[s, g - 1])
        if halos:
            mine = [
                [dot(there[s, :, lanes_of(edges[side])], whalo[side, s]) for side in range(2)]
                for s in range(segs)
            ]
        if not finish:
            force_into([(moved[s, g], slope_of(s, g), s, g) for s in range(segs) for g in inner], there)
        if not halos:
            send()
        if halos:
            for side in range(2):
                arrival(n - 1, side).wait()
            force_into(
                [
                    (mine[s][side] + came[n - 1, side, s].astype(jnp.float32), slope_beyond(s, side), s, halo[side])
                    for s in range(segs)
                    for side in range(2)
                ],
                here,
            )
        for side in range(2):
            g = edges[side]
            for s in range(segs):
                moved[s, g] = own[s][side] + dot(
                    here[s, :, lanes_of(halo[side])], w_edge[s, side, side * 2 * pair:(side * 2 + 1) * pair, :]
                )
        if finish:
            for s in range(segs):
                for g in range(pairs):
                    for j in range(2):
                        orth_ref[pl.ds(s * per + 2 * g + j, tracers, stride=rows), :] = (
                            moved[s, g][:tracers, j * points:(j + 1) * points]
                        )
        else:
            force_into([(moved[s, g], slope_of(s, g), s, g) for s in range(segs) for g in edges], there)

    step(0, 0, False, False)
    follow_copy.start()
    for x in gram_copies1:
        x.start()

    def two(i, unused):
        step(2 * i + 1, 1, True, False)
        step(2 * i + 2, 0, True, False)
        return unused

    lax.fori_loop(0, (STEPS - 2) // 2, two, 0)
    step(STEPS - 1, 1, True, True)

    gram2[me_seg] = total_of(gram1, gram_copies1, n_blk)
    gram_copies2 = everyone(gram2, me_seg, "seg", n_seg, gram_sem2)
    for x in gram_copies2:
        x.start()
    follow_copy.wait()

    def project(i, acc):
        here = pl.ds(pl.multiple_of(i * rows, rows), rows)
        for s in range(segs):
            at = pl.ds(pl.multiple_of(i * rows, rows) + s * per, rows)
            if s < segs - 1:
                nxt = dir_ref[pl.ds(pl.multiple_of(i * rows, rows) + (s + 1) * per, rows), :]
            else:
                nxt = follow[here, :]
            shot = orth_ref[at, :] - nxt
            orth_ref[at, :] = shot
            acc = tuple(acc[j] + basis[j, at, :] * shot for j in range(kry)) + (acc[kry] + shot * shot,)
        return acc

    sums = lax.fori_loop(0, tracers, project, (zero,) * (kry + 1), unroll=4)
    for j in range(kry):
        part1[me_blk, pl.ds(j, 1), :] = fold(sums[j])
    part1[me_blk, pl.ds(8, 8), :] = sums[kry]

    copies = everyone(part1, me_blk, "blk", n_blk, red_sem1)
    for x in copies:
        x.start()
    part2[me_seg] = total_of(part1, copies, n_blk)
    copies = everyone(part2, me_seg, "seg", n_seg, red_sem2)
    for x in copies:
        x.start()
    gramd = jnp.sum(total_of(gram2, gram_copies2, n_seg), axis=1, keepdims=True)
    sumd = jnp.sum(total_of(part2, copies, n_seg), axis=1, keepdims=True)
    h = sumd[0:kry]
    hv = [sumd[j:j + 1] for j in range(kry)]
    quad = jnp.zeros((kry, 1), jnp.float32)
    for m in range(half):
        turned = h if m == 0 else jnp.concatenate([h[m:], h[:m]], axis=0)
        weight = 1.0 if m == 0 or 2 * m == kry else 2.0
        quad = quad + weight * (turned * gramd[m * 8:m * 8 + kry])
    quad = h * (quad - 2.0 * h) + sumd[8:16]
    square = jnp.sum(jnp.broadcast_to(quad, (kry, points)), axis=0, keepdims=True)
    length = jnp.sqrt(jnp.maximum(square, 0.0) / entries)
    coef_ref[kry] = length[0, 0]
    for j in range(kry):
        coef_ref[j] = hv[j][0, 0]
    wide = [jnp.broadcast_to(x, (rows, points)) for x in hv]

    def subtract(i, unused):
        at = pl.ds(pl.multiple_of(i * rows, rows), rows)
        a = hv_sum([wide[j] * basis[j, at, :] for j in range(kry)])
        orth_ref[at, :] = orth_ref[at, :] - a
        return unused

    lax.fori_loop(0, chunks, subtract, 0, unroll=4)


def hv_sum(terms):
    while len(terms) > 1:
        terms = [sum(terms[i:i + 2]) for i in range(0, len(terms), 2)]
    return terms[0]


def on_device(n_seg, n_blk, base_state, direction, coupling, tiles, columns, wet, basis):
    segs, tracers, rows, points = direction.shape
    stored = tiles.shape[2]
    kry = basis.shape[0]
    total = rows * n_blk
    entries = float(segs * n_seg * tracers * total * points)
    pairs = rows // 2
    pair = 2 * points
    wide = 2 * REACH + 2
    flat = segs * tracers * rows
    base_flat = base_state.reshape(flat, points)
    dir_flat = direction.reshape(flat, points)
    basis_flat = basis.reshape(kry, flat, points)
    in_vmem = pl.BlockSpec(memory_space=pltpu.VMEM)
    in_hbm = pl.BlockSpec(memory_space=pltpu.HBM)
    bf16, f32 = jnp.bfloat16, jnp.float32
    shape = jax.ShapeDtypeStruct

    def scratch_of(count):
        return [
            pltpu.SMEM((segs, rows, stored), jnp.int32),
            pltpu.VMEM((rows, points), jnp.int32),
            pltpu.VMEM((segs, 2 * count, stored, points, points), bf16),
            pltpu.VMEM((2 * REACH + 1, points, points), f32),
            pltpu.VMEM((2 * REACH + 1, points, points), f32),
        ]

    def sems_of(count):
        return [pltpu.SemaphoreType.DMA((2,)), pltpu.SemaphoreType.DMA((segs, 2 * count))]

    dims = (segs, tracers, rows, points, total)
    work = segs * rows * stored * points * points
    border = shape((segs, 3 * points + 6 * PAD, points), bf16)
    w_edge, slope, start, to_left, to_right = pl.pallas_call(
        functools.partial(edge_kernel, dims),
        out_shape=(
            shape((segs, 2, wide * points, pair), bf16), shape((segs, PAD, rows * points), f32),
            shape((segs, PAD, rows * points), bf16), border, border,
        ),
        in_specs=[in_hbm] * 6,
        out_specs=(in_hbm,) * 5,
        scratch_shapes=scratch_of(2) + [
            pltpu.VMEM((PAD, 2 * PAD), f32),
            pltpu.VMEM((flat, points), f32),
            pltpu.VMEM((flat, points), f32),
            pltpu.VMEM((tracers, tracers), f32),
            pltpu.VMEM((segs, 2, wide * points, pair), bf16),
            pltpu.VMEM((segs, PAD, rows * points), f32),
            pltpu.VMEM((segs, PAD, rows * points), bf16),
            pltpu.VMEM((2, segs, 3 * points + 6 * PAD, points), bf16),
        ] + sems_of(2) + [
            pltpu.SemaphoreType.DMA((3,)),
            pltpu.SemaphoreType.DMA((segs, 2)),
            pltpu.SemaphoreType.DMA((4,)),
        ],
        compiler_params=pltpu.CompilerParams(vmem_limit_bytes=48 << 20),
        cost_estimate=pl.CostEstimate(flops=8 * work, bytes_accessed=work, transcendentals=0),
        name="edge",
    )(base_flat, dir_flat, coupling, columns, wet, tiles)
    ring = range(n_blk)
    from_right = lax.ppermute(to_left, "blk", [(i, (i + n_blk - 1) % n_blk) for i in ring])
    from_left = lax.ppermute(to_right, "blk", [(i, (i + 1) % n_blk) for i in ring])
    w_inner, gram = pl.pallas_call(
        functools.partial(inner_kernel, dims),
        out_shape=(
            shape((segs, pairs - 2, wide * points, pair), bf16), shape(((kry // 2 + 1) * 8, points), f32),
        ),
        in_specs=[in_vmem] + [in_hbm] * 3,
        out_specs=(in_vmem,) * 2,
        scratch_shapes=scratch_of(pairs - 2) + sems_of(pairs - 2),
        compiler_params=pltpu.CompilerParams(vmem_limit_bytes=48 << 20),
        cost_estimate=pl.CostEstimate(flops=8 * work, bytes_accessed=work, transcendentals=0),
        name="inner",
    )(basis_flat, columns, wet, tiles)
    dims = (segs, tracers, rows, points, kry, n_seg, n_blk, entries)
    half = (kry // 2 + 1) * 8
    orth, coef = pl.pallas_call(
        functools.partial(steps_kernel, dims),
        out_shape=(
            jax.ShapeDtypeStruct((flat, points), jnp.float32),
            jax.ShapeDtypeStruct((kry + 1,), jnp.float32),
        ),
        in_specs=[in_vmem] * 10,
        out_specs=(in_vmem, pl.BlockSpec(memory_space=pltpu.SMEM)),
        scratch_shapes=[
            pltpu.VMEM((segs, PAD, (pairs + 2) * pair), jnp.bfloat16),
            pltpu.VMEM((segs, PAD, (pairs + 2) * pair), jnp.bfloat16),
            pltpu.VMEM((PAD, 2 * PAD), jnp.float32),
            pltpu.VMEM((tracers * rows, points), jnp.float32),
            pltpu.VMEM((2, segs, pair, pair), jnp.bfloat16),
            pltpu.VMEM((STEPS - 1, 2, segs, PAD, pair), jnp.bfloat16),
            pltpu.VMEM((STEPS - 1, 2, segs, PAD, pair), jnp.bfloat16),
            pltpu.VMEM((n_blk, 16, points), jnp.float32),
            pltpu.VMEM((n_seg, 16, points), jnp.float32),
            pltpu.VMEM((n_blk, half, points), jnp.float32),
            pltpu.VMEM((n_seg, half, points), jnp.float32),
            pltpu.SemaphoreType.DMA((STEPS - 1, 2)),
            pltpu.SemaphoreType.DMA((STEPS - 1, 2)),
            pltpu.SemaphoreType.DMA((2,)),
            pltpu.SemaphoreType.DMA((2, n_blk - 1)),
            pltpu.SemaphoreType.DMA((2, n_seg - 1)),
            pltpu.SemaphoreType.DMA((2, n_blk - 1)),
            pltpu.SemaphoreType.DMA((2, n_seg - 1)),
        ],
        compiler_params=pltpu.CompilerParams(
            collective_id=0, has_side_effects=True, vmem_limit_bytes=40 << 20
        ),
        name="steps",
    )(slope, start, dir_flat, coupling, w_edge, w_inner, from_left, from_right, gram, basis_flat)
    return orth.reshape(direction.shape), coef


def solution(mesh):
    in_specs = (
        P(("groups", "seg"), None, "blk", None),
        P(("groups", "seg"), None, "blk", None),
        P("groups", None),
        P("seg", "blk", None, None, None),
        P("seg", "blk", None),
        P("blk", None),
        P(None, ("groups", "seg"), None, "blk", None),
    )
    out_specs = (P(("groups", "seg"), None, "blk", None), P("groups"))
    body = functools.partial(on_device, mesh.shape["seg"], mesh.shape["blk"])
    return jax.shard_map(body, mesh=mesh, in_specs=in_specs, out_specs=out_specs, check_vma=False)
```

```python
import functools

import jax
import jax.numpy as jnp
from jax import lax
from jax.experimental import pallas as pl
from jax.experimental.pallas import tpu as pltpu
from jax.sharding import PartitionSpec as P

STEPS = 18
SWITCH = 5
MESH = pl.DeviceIdType.MESH
REACH = 2
PAD = 32
BATCH = 4
BORDER = (((0, 0), (1, 0), (1, 1)), ((0, 0), (0, 1), (1, 1)))


def merge_pair(total, first, stored, row, cols_at, tile_at, wet, accs, put):
    wide = 2 * REACH + 1
    for acc in accs:
        acc[...] = jnp.zeros_like(acc)

    def add(k, unused):
        for j in range(2):
            col = cols_at(row + j, k)
            d = lax.rem(col - first - row - j + (REACH + total), total)
            accs[j][d] += tile_at(j, k).astype(jnp.float32)
        return unused

    lax.fori_loop(0, stored, add, 0, unroll=4)
    size = accs[0].shape[1]
    for j in range(2):
        mask = wet(row + j).astype(jnp.float32)
        for c in range(wide + 1):
            d = c - j
            if 0 <= d < wide:
                put(c, j, (accs[j][d].T * mask).astype(jnp.bfloat16))
            else:
                put(c, j, jnp.zeros((size, size), jnp.bfloat16))


def merge_pairs(total, rows, groups, cols, wet_v, tile_buf, waits, accs, w_ref, then=None):
    first = lax.axis_index("blk") * rows
    segs = cols.shape[0]
    size = accs[0].shape[1]
    for i, g in enumerate(groups):
        for s in range(segs):
            for x in waits[i * segs + s]:
                x.wait()

            def put(c, j, part):
                w_ref[s, i, c * size:(c + 1) * size, j * size:(j + 1) * size] = part

            merge_pair(
                total, first, cols.shape[2], 2 * g, lambda row, k: cols[s, row, k],
                lambda j, k: tile_buf[s, 2 * i + j, k],
                lambda row: wet_v[pl.ds(row, 1), :], accs, put,
            )
            if then is not None:
                then(i, s)


def start_fetches(groups, cols_ref, wet_ref, tiles_ref, cols, wet_v, tile_buf, small_sem, tile_sem):
    small = [
        pltpu.make_async_copy(cols_ref, cols, small_sem.at[0]),
        pltpu.make_async_copy(wet_ref, wet_v, small_sem.at[1]),
    ]
    waits = []
    for i, g in enumerate(groups):
        for s in range(cols_ref.shape[0]):
            waits.append(
                [
                    pltpu.make_async_copy(
                        tiles_ref.at[s, 2 * g + j], tile_buf.at[s, 2 * i + j], tile_sem.at[s, 2 * i + j]
                    )
                    for j in range(2)
                ]
            )
    for x in small:
        x.start()
    for both in waits:
        for x in both:
            x.start()
    return small, waits


def mix_of(coup_ref, cc):
    tracers = coup_ref.shape[0]
    c = 0.5 * coup_ref[...]
    high = c.astype(jnp.bfloat16)
    low = (c - high.astype(jnp.float32)).astype(jnp.bfloat16)
    cc[...] = jnp.zeros_like(cc)
    cc[:tracers, 0:tracers] = high.astype(jnp.float32)
    cc[:tracers, PAD:PAD + tracers] = low.astype(jnp.float32)
    one = cc[...]
    blank = jnp.zeros_like(one)
    return jnp.concatenate(
        [
            jnp.concatenate([one if i == j else blank for j in range(BATCH)], axis=1)
            for i in range(BATCH)
        ],
        axis=0,
    ).astype(jnp.bfloat16)


def dot(a, b):
    return jnp.dot(a, b, preferred_element_type=jnp.float32)


def forced(mix, us, ks):
    out = []
    for i in range(0, len(us), BATCH):
        group = us[i:i + BATCH]
        n = len(group)
        xs = [(k * u).astype(jnp.bfloat16) for u, k in zip(group, ks[i:i + BATCH])]
        stack = jnp.concatenate([x for x in xs for unused in range(2)], axis=0)
        added = dot(mix[:n * PAD, :2 * n * PAD], stack)
        out += [(u + added[j * PAD:(j + 1) * PAD]).astype(jnp.bfloat16) for j, u in enumerate(group)]
    return out


def edge_kernel(
    dims, base_hbm, dir_hbm, coup_hbm, cols_ref, wet_ref, tiles_ref, w_ref, slope_ref, drive_ref, left_ref, right_ref,
    cols, wet_v, tile_buf, acc0, acc1, cc, base, direction, coup, w_v, slope_v, drive_v, out_v,
    small_sem, tile_sem, in_sem, w_sem, out_sem,
):
    segs, tracers, rows, points, total = dims
    pairs = rows // 2
    per = tracers * rows
    pair = 2 * points
    edges = (0, pairs - 1)
    fetches = [
        pltpu.make_async_copy(a, b, in_sem.at[i])
        for i, (a, b) in enumerate([(base_hbm, base), (dir_hbm, direction), (coup_hbm, coup)])
    ]
    for x in fetches:
        x.start()
    small, waits = start_fetches(edges, cols_ref, wet_ref, tiles_ref, cols, wet_v, tile_buf, small_sem, tile_sem)
    for x in fetches:
        x.wait()
    mix = mix_of(coup, cc)

    def native(ref, s, g):
        halves = [
            jnp.concatenate(
                [
                    ref[pl.ds(s * per + 2 * g + j, tracers, stride=rows), :],
                    jnp.zeros((PAD - tracers, points), jnp.float32),
                ],
                axis=0,
            )
            for j in range(2)
        ]
        return jnp.concatenate(halves, axis=1)

    units = [(s, g) for s in range(segs) for g in range(pairs)]
    slopes, starts = [], []
    for s, g in units:
        t = jnp.tanh(native(base, s, g))
        k = 1.0 - t * t
        slope_v[s, :, g * pair:(g + 1) * pair] = k
        slopes.append(k)
        starts.append(native(direction, s, g))
    drives = forced(mix, starts, slopes)
    for (s, g), d, k in zip(units, drives, slopes):
        drive_v[s, :, g * pair:(g + 1) * pair] = d
        if g in edges:
            high = k.astype(jnp.bfloat16)
            low = (k - high.astype(jnp.float32)).astype(jnp.bfloat16)
            for i, x in enumerate((d, high, low)):
                for j in range(2):
                    at = 3 * points + (2 * i + j) * PAD
                    out_v[edges.index(g), s, at:at + PAD, :] = x[:, j * points:(j + 1) * points]
    for x in small:
        x.wait()
    outs = [
        pltpu.make_async_copy(slope_v, slope_ref, out_sem.at[0]),
        pltpu.make_async_copy(drive_v, drive_ref, out_sem.at[1]),
    ]
    for x in outs:
        x.start()

    def merged(i, s):
        for n, (c, j) in enumerate(BORDER[i]):
            c = c + i * 2 * REACH
            out_v[i, s, n * points:(n + 1) * points, :] = (
                w_v[s, i, c * points:(c + 1) * points, j * points:(j + 1) * points]
            )
        copy = pltpu.make_async_copy(w_v.at[s, i], w_ref.at[s, i], w_sem.at[s, i])
        copy.start()
        outs.append(copy)
        if s == segs - 1:
            copy = pltpu.make_async_copy(out_v.at[i], (left_ref, right_ref)[i], out_sem.at[2 + i])
            copy.start()
            outs.append(copy)

    merge_pairs(total, rows, edges, cols, wet_v, tile_buf, waits, (acc0, acc1), w_v, merged)
    for x in outs:
        x.wait()


def inner_kernel(
    dims, basis, cols_ref, wet_ref, tiles_ref, w_ref, gram_ref,
    cols, wet_v, tile_buf, acc0, acc1, small_sem, tile_sem,
):
    segs, tracers, rows, points, total = dims
    pairs = rows // 2
    kry = basis.shape[0]
    groups = tuple(range(1, pairs - 1))
    small, waits = start_fetches(groups, cols_ref, wet_ref, tiles_ref, cols, wet_v, tile_buf, small_sem, tile_sem)
    half = kry // 2 + 1

    def gram(i, acc):
        b = [basis[j, pl.ds(pl.multiple_of(i * rows, rows), rows), :] for j in range(kry)]
        return tuple(acc[m * kry + j] + b[j] * b[(j + m) % kry] for m in range(half) for j in range(kry))

    zero = jnp.zeros((rows, points), jnp.float32)
    sums = lax.fori_loop(0, segs * tracers, gram, (zero,) * (half * kry))
    for m in range(half):
        for j in range(kry):
            gram_ref[pl.ds(m * 8 + j, 1), :] = jnp.sum(sums[m * kry + j], axis=0, keepdims=True)
    for x in small:
        x.wait()
    merge_pairs(total, rows, groups, cols, wet_v, tile_buf, waits, (acc0, acc1), w_ref)


def steps_kernel(
    dims, slope, start, dir_ref, coup_ref, w_edge, w_inner, from_left, from_right, gram_in, basis, orth_ref, coef_ref,
    drive0, drive1, cc, follow, whalo, whalo2, hold, sent, came, part1, part2, gram1, gram2,
    send_sem, recv_sem, border_send, border_recv, follow_sem, red_sem1, red_sem2, gram_sem1, gram_sem2,
):
    segs, tracers, rows, points, kry, n_seg, n_blk, entries = dims
    pairs = rows // 2
    per = tracers * rows
    pair = 2 * points
    drive = (drive0, drive1)
    me_seg, me_blk = lax.axis_index("seg"), lax.axis_index("blk")
    left, right = lax.rem(me_blk + n_blk - 1, n_blk), lax.rem(me_blk + 1, n_blk)

    barrier = pltpu.get_barrier_semaphore()
    for i in range(1, n_blk):
        pl.semaphore_signal(barrier, inc=1, device_id={"blk": lax.rem(me_blk + i, n_blk)}, device_id_type=MESH)
    for i in range(1, n_seg):
        pl.semaphore_signal(barrier, inc=1, device_id={"seg": lax.rem(me_seg + i, n_seg)}, device_id_type=MESH)

    def lanes_of(g, count=1):
        return slice((g + 1) * pair, (g + 1 + count) * pair)

    mix = mix_of(coup_ref, cc)
    halos_in = (from_left, from_right)

    def force_into(units, to):
        values = forced(mix, [u for u, k, s, g in units], [k for u, k, s, g in units])
        for (u, k, s, g), v in zip(units, values):
            to[s, :, lanes_of(g)] = v

    def slope_of(s, g):
        return slope[s, :, g * pair:(g + 1) * pair]

    def beyond(s, side, i):
        at = 3 * points + 2 * i * PAD
        ref = halos_in[side]
        return jnp.concatenate([ref[s, at:at + PAD, :], ref[s, at + PAD:at + 2 * PAD, :]], axis=1)

    def slope_beyond(s, side):
        return beyond(s, side, 1).astype(jnp.float32) + beyond(s, side, 2).astype(jnp.float32)

    edges = (0, pairs - 1)
    inner = range(1, pairs - 1)
    halo = (-1, pairs)
    for s in range(segs):
        drive0[s, :, pair:(pairs + 1) * pair] = start[s]
        for side in range(2):
            drive0[s, :, lanes_of(halo[side])] = beyond(s, side, 0)
            whalo[side, s] = jnp.zeros((pair, pair), jnp.bfloat16)
            for n, (c, j) in enumerate(BORDER[1 - side]):
                whalo[side, s, c * points:(c + 1) * points, j * points:(j + 1) * points] = (
                    halos_in[side][s, n * points:(n + 1) * points, :]
                )
    gram1[me_blk] = gram_in[...]
    follow_copy = pltpu.make_async_remote_copy(
        src_ref=dir_ref.at[0:per], dst_ref=follow, send_sem=follow_sem.at[0], recv_sem=follow_sem.at[1],
        device_id={"seg": lax.rem(me_seg + n_seg - 1, n_seg)}, device_id_type=MESH,
    )
    chunks = segs * tracers
    half = kry // 2 + 1

    def fold(a):
        return jnp.sum(a, axis=0, keepdims=True)

    def everyone(part, me, axis, count, sems):
        return [
            pltpu.make_async_remote_copy(
                src_ref=part.at[me], dst_ref=part.at[me],
                send_sem=sems.at[0, i - 1], recv_sem=sems.at[1, i - 1],
                device_id={axis: lax.rem(me + i, count)}, device_id_type=MESH,
            )
            for i in range(1, count)
        ]

    def total_of(part, copies, count):
        for x in copies:
            x.wait()
        result = part[0]
        for i in range(1, count):
            result = result + part[i]
        return result

    zero = jnp.zeros((rows, points), jnp.float32)
    gram_copies1 = everyone(gram1, me_blk, "blk", n_blk, gram_sem1)

    def message(n, side):
        return pltpu.make_async_remote_copy(
            src_ref=sent.at[n, side], dst_ref=came.at[n, 1 - side],
            send_sem=send_sem.at[n, side], recv_sem=recv_sem.at[n, 1 - side],
            device_id={"blk": (left, right)[side]}, device_id_type=MESH,
        )

    def arrival(n, side):
        return pltpu.make_async_remote_copy(
            src_ref=sent.at[n, 1 - side], dst_ref=came.at[n, side],
            send_sem=send_sem.at[n, 1 - side], recv_sem=recv_sem.at[n, side],
            device_id={"blk": (left, right)[1 - side]}, device_id_type=MESH,
        )

    def step(n, slot, halos, pieces):
        here, there = drive[slot], drive[1 - slot]
        own = [[None, None] for s in range(segs)]
        for s in range(segs):
            own[s][0] = dot(here[s, :, lanes_of(0, 2)], w_edge[s, 0, pair:3 * pair, :])
            own[s][1] = dot(here[s, :, lanes_of(pairs - 2, 2)], w_edge[s, 1, 0:2 * pair, :])
        def send():
            for side in range(2):
                for s in range(segs):
                    sent[n, side, s] = own[s][side].astype(jnp.bfloat16)
            if not halos:
                pl.semaphore_wait(barrier, n_blk + n_seg - 2)
            for side in range(2):
                message(n, side).start()
            for x in pieces:
                x.start()

        if halos:
            send()
        moved = {}
        for s in range(segs):
            for g in range(1, pairs - 1):
                moved[s, g] = dot(here[s, :, lanes_of(g - 1, 3)], w_inner[s, g - 1])
        if halos:
            mine = [
                [dot(there[s, :, lanes_of(edges[side])], whalo[side, s]) for side in range(2)]
                for s in range(segs)
            ]
        force_into([(moved[s, g], slope_of(s, g), s, g) for s in range(segs) for g in inner], there)
        if not halos:
            send()
        if halos:
            for side in range(2):
                arrival(n - 1, side).wait()
            force_into(
                [
                    (mine[s][side] + came[n - 1, side, s].astype(jnp.float32), slope_beyond(s, side), s, halo[side])
                    for s in range(segs)
                    for side in range(2)
                ],
                here,
            )
        for side in range(2):
            g = edges[side]
            for s in range(segs):
                moved[s, g] = own[s][side] + dot(
                    here[s, :, lanes_of(halo[side])], w_edge[s, side, side * 2 * pair:(side * 2 + 1) * pair, :]
                )
        force_into([(moved[s, g], slope_of(s, g), s, g) for s in range(segs) for g in edges], there)

    def beside(n, slot):
        here = drive[slot]
        for s in range(segs):
            r = (
                dot(here[s, :, lanes_of(1)], w_edge[s, 0, 2 * pair:3 * pair, :]),
                dot(here[s, :, lanes_of(pairs - 2)], w_edge[s, 1, 0:pair, :]),
            )
            for side in range(2):
                hold[slot, s, side] = r[side]
                sent[n, side, s] = r[side].astype(jnp.bfloat16)
        for side in range(2):
            message(n, side).start()

    def late_step(n, slot, finish):
        here, there = drive[slot], drive[1 - slot]
        moved = {}
        for s in range(segs):
            for g in inner:
                moved[s, g] = dot(here[s, :, lanes_of(g - 1, 3)], w_inner[s, g - 1])
        mine = {}
        for s in range(segs):
            for side in range(2):
                old = dot(there[s, :, lanes_of(halo[side])], whalo2[side, s])
                mine[s, side] = (
                    dot(there[s, :, lanes_of(edges[side])], whalo[side, s]) + jnp.where(n > SWITCH, old, 0.0)
                )
        if not finish:
            force_into([(moved[s, g], slope_of(s, g), s, g) for s in range(segs) for g in inner], there)
            beside(n + 1, 1 - slot)
        for side in range(2):
            arrival(n - 1, side).wait()
        force_into(
            [
                (mine[s, side] + came[n - 1, side, s].astype(jnp.float32), slope_beyond(s, side), s, halo[side])
                for s in range(segs)
                for side in range(2)
            ],
            here,
        )
        for side in range(2):
            g = edges[side]
            for s in range(segs):
                moved[s, g] = hold[slot, s, side] + dot(
                    here[s, :, lanes_of((-1, pairs - 1)[side], 2)], w_edge[s, side, side * pair:(side + 2) * pair, :]
                )
        if finish:
            for s in range(segs):
                for g in range(pairs):
                    for j in range(2):
                        orth_ref[pl.ds(s * per + 2 * g + j, tracers, stride=rows), :] = (
                            moved[s, g][:tracers, j * points:(j + 1) * points]
                        )
        else:
            force_into([(moved[s, g], slope_of(s, g), s, g) for s in range(segs) for g in edges], there)

    count = (SWITCH - 1) // segs
    size = pair // count
    borders = [
        [
            pltpu.make_async_remote_copy(
                src_ref=w_edge.at[s, side, pair + k * size:pair + (k + 1) * size, :],
                dst_ref=whalo2.at[1 - side, s, k * size:(k + 1) * size, :],
                send_sem=border_send.at[s * count + k, side], recv_sem=border_recv.at[s * count + k, side],
                device_id={"blk": (left, right)[side]}, device_id_type=MESH,
            )
            for side in range(2)
        ]
        for s in range(segs)
        for k in range(count)
    ]
    for n in range(SWITCH):
        step(n, n % 2, n > 0, borders[n] if n < len(borders) else [])
    follow_copy.start()
    for x in gram_copies1:
        x.start()
    beside(SWITCH, 1)
    for both in borders:
        for x in both:
            x.wait()

    def two_late(i, unused):
        late_step(SWITCH + 2 * i, 1, False)
        late_step(SWITCH + 2 * i + 1, 0, False)
        return unused

    lax.fori_loop(0, (STEPS - 1 - SWITCH) // 2, two_late, 0)
    late_step(STEPS - 1, 1, True)

    gram2[me_seg] = total_of(gram1, gram_copies1, n_blk)
    gram_copies2 = everyone(gram2, me_seg, "seg", n_seg, gram_sem2)
    for x in gram_copies2:
        x.start()
    follow_copy.wait()

    def project(i, acc):
        here = pl.ds(pl.multiple_of(i * rows, rows), rows)
        for s in range(segs):
            at = pl.ds(pl.multiple_of(i * rows, rows) + s * per, rows)
            if s < segs - 1:
                nxt = dir_ref[pl.ds(pl.multiple_of(i * rows, rows) + (s + 1) * per, rows), :]
            else:
                nxt = follow[here, :]
            shot = orth_ref[at, :] - nxt
            orth_ref[at, :] = shot
            acc = tuple(acc[j] + basis[j, at, :] * shot for j in range(kry)) + (acc[kry] + shot * shot,)
        return acc

    sums = lax.fori_loop(0, tracers, project, (zero,) * (kry + 1), unroll=4)
    for j in range(kry):
        part1[me_blk, pl.ds(j, 1), :] = fold(sums[j])
    part1[me_blk, pl.ds(8, 8), :] = sums[kry]

    copies = everyone(part1, me_blk, "blk", n_blk, red_sem1)
    for x in copies:
        x.start()
    for side in range(2):
        arrival(STEPS - 1, side).wait()
    part2[me_seg] = total_of(part1, copies, n_blk)
    copies = everyone(part2, me_seg, "seg", n_seg, red_sem2)
    for x in copies:
        x.start()
    gramd = jnp.sum(total_of(gram2, gram_copies2, n_seg), axis=1, keepdims=True)
    sumd = jnp.sum(total_of(part2, copies, n_seg), axis=1, keepdims=True)
    h = sumd[0:kry]
    hv = [sumd[j:j + 1] for j in range(kry)]
    quad = jnp.zeros((kry, 1), jnp.float32)
    for m in range(half):
        turned = h if m == 0 else jnp.concatenate([h[m:], h[:m]], axis=0)
        weight = 1.0 if m == 0 or 2 * m == kry else 2.0
        quad = quad + weight * (turned * gramd[m * 8:m * 8 + kry])
    quad = h * (quad - 2.0 * h) + sumd[8:16]
    square = jnp.sum(jnp.broadcast_to(quad, (kry, points)), axis=0, keepdims=True)
    length = jnp.sqrt(jnp.maximum(square, 0.0) / entries)
    coef_ref[kry] = length[0, 0]
    for j in range(kry):
        coef_ref[j] = hv[j][0, 0]
    wide = [jnp.broadcast_to(x, (rows, points)) for x in hv]

    def subtract(i, unused):
        at = pl.ds(pl.multiple_of(i * rows, rows), rows)
        a = hv_sum([wide[j] * basis[j, at, :] for j in range(kry)])
        orth_ref[at, :] = orth_ref[at, :] - a
        return unused

    lax.fori_loop(0, chunks, subtract, 0, unroll=4)


def hv_sum(terms):
    while len(terms) > 1:
        terms = [sum(terms[i:i + 2]) for i in range(0, len(terms), 2)]
    return terms[0]


def on_device(n_seg, n_blk, base_state, direction, coupling, tiles, columns, wet, basis):
    segs, tracers, rows, points = direction.shape
    stored = tiles.shape[2]
    kry = basis.shape[0]
    total = rows * n_blk
    entries = float(segs * n_seg * tracers * total * points)
    pairs = rows // 2
    pair = 2 * points
    wide = 2 * REACH + 2
    flat = segs * tracers * rows
    base_flat = base_state.reshape(flat, points)
    dir_flat = direction.reshape(flat, points)
    basis_flat = basis.reshape(kry, flat, points)
    in_vmem = pl.BlockSpec(memory_space=pltpu.VMEM)
    in_hbm = pl.BlockSpec(memory_space=pltpu.HBM)
    bf16, f32 = jnp.bfloat16, jnp.float32
    shape = jax.ShapeDtypeStruct

    def scratch_of(count):
        return [
            pltpu.SMEM((segs, rows, stored), jnp.int32),
            pltpu.VMEM((rows, points), jnp.int32),
            pltpu.VMEM((segs, 2 * count, stored, points, points), bf16),
            pltpu.VMEM((2 * REACH + 1, points, points), f32),
            pltpu.VMEM((2 * REACH + 1, points, points), f32),
        ]

    def sems_of(count):
        return [pltpu.SemaphoreType.DMA((2,)), pltpu.SemaphoreType.DMA((segs, 2 * count))]

    dims = (segs, tracers, rows, points, total)
    work = segs * rows * stored * points * points
    border = shape((segs, 3 * points + 6 * PAD, points), bf16)
    w_edge, slope, start, to_left, to_right = pl.pallas_call(
        functools.partial(edge_kernel, dims),
        out_shape=(
            shape((segs, 2, wide * points, pair), bf16), shape((segs, PAD, rows * points), f32),
            shape((segs, PAD, rows * points), bf16), border, border,
        ),
        in_specs=[in_hbm] * 6,
        out_specs=(in_hbm,) * 5,
        scratch_shapes=scratch_of(2) + [
            pltpu.VMEM((PAD, 2 * PAD), f32),
            pltpu.VMEM((flat, points), f32),
            pltpu.VMEM((flat, points), f32),
            pltpu.VMEM((tracers, tracers), f32),
            pltpu.VMEM((segs, 2, wide * points, pair), bf16),
            pltpu.VMEM((segs, PAD, rows * points), f32),
            pltpu.VMEM((segs, PAD, rows * points), bf16),
            pltpu.VMEM((2, segs, 3 * points + 6 * PAD, points), bf16),
        ] + sems_of(2) + [
            pltpu.SemaphoreType.DMA((3,)),
            pltpu.SemaphoreType.DMA((segs, 2)),
            pltpu.SemaphoreType.DMA((4,)),
        ],
        compiler_params=pltpu.CompilerParams(vmem_limit_bytes=56 << 20),
        cost_estimate=pl.CostEstimate(flops=8 * work, bytes_accessed=work, transcendentals=0),
        name="edge",
    )(base_flat, dir_flat, coupling, columns, wet, tiles)
    ring = range(n_blk)
    from_right = lax.ppermute(to_left, "blk", [(i, (i + n_blk - 1) % n_blk) for i in ring])
    from_left = lax.ppermute(to_right, "blk", [(i, (i + 1) % n_blk) for i in ring])
    w_inner, gram = pl.pallas_call(
        functools.partial(inner_kernel, dims),
        out_shape=(
            shape((segs, pairs - 2, wide * points, pair), bf16), shape(((kry // 2 + 1) * 8, points), f32),
        ),
        in_specs=[in_vmem] + [in_hbm] * 3,
        out_specs=(in_vmem,) * 2,
        scratch_shapes=scratch_of(pairs - 2) + sems_of(pairs - 2),
        compiler_params=pltpu.CompilerParams(vmem_limit_bytes=48 << 20),
        cost_estimate=pl.CostEstimate(flops=8 * work, bytes_accessed=work, transcendentals=0),
        name="inner",
    )(basis_flat, columns, wet, tiles)
    dims = (segs, tracers, rows, points, kry, n_seg, n_blk, entries)
    half = (kry // 2 + 1) * 8
    orth, coef = pl.pallas_call(
        functools.partial(steps_kernel, dims),
        out_shape=(
            jax.ShapeDtypeStruct((flat, points), jnp.float32),
            jax.ShapeDtypeStruct((kry + 1,), jnp.float32),
        ),
        in_specs=[in_vmem] * 10,
        out_specs=(in_vmem, pl.BlockSpec(memory_space=pltpu.SMEM)),
        scratch_shapes=[
            pltpu.VMEM((segs, PAD, (pairs + 2) * pair), jnp.bfloat16),
            pltpu.VMEM((segs, PAD, (pairs + 2) * pair), jnp.bfloat16),
            pltpu.VMEM((PAD, 2 * PAD), jnp.float32),
            pltpu.VMEM((tracers * rows, points), jnp.float32),
            pltpu.VMEM((2, segs, pair, pair), jnp.bfloat16),
            pltpu.VMEM((2, segs, pair, pair), jnp.bfloat16),
            pltpu.VMEM((2, segs, 2, PAD, pair), jnp.float32),
            pltpu.VMEM((STEPS, 2, segs, PAD, pair), jnp.bfloat16),
            pltpu.VMEM((STEPS, 2, segs, PAD, pair), jnp.bfloat16),
            pltpu.VMEM((n_blk, 16, points), jnp.float32),
            pltpu.VMEM((n_seg, 16, points), jnp.float32),
            pltpu.VMEM((n_blk, half, points), jnp.float32),
            pltpu.VMEM((n_seg, half, points), jnp.float32),
            pltpu.SemaphoreType.DMA((STEPS, 2)),
            pltpu.SemaphoreType.DMA((STEPS, 2)),
            pltpu.SemaphoreType.DMA((SWITCH - 1, 2)),
            pltpu.SemaphoreType.DMA((SWITCH - 1, 2)),
            pltpu.SemaphoreType.DMA((2,)),
            pltpu.SemaphoreType.DMA((2, n_blk - 1)),
            pltpu.SemaphoreType.DMA((2, n_seg - 1)),
            pltpu.SemaphoreType.DMA((2, n_blk - 1)),
            pltpu.SemaphoreType.DMA((2, n_seg - 1)),
        ],
        compiler_params=pltpu.CompilerParams(
            collective_id=0, has_side_effects=True, vmem_limit_bytes=40 << 20
        ),
        name="steps",
    )(slope, start, dir_flat, coupling, w_edge, w_inner, from_left, from_right, gram, basis_flat)
    return orth.reshape(direction.shape), coef


def solution(mesh):
    in_specs = (
        P(("groups", "seg"), None, "blk", None),
        P(("groups", "seg"), None, "blk", None),
        P("groups", None),
        P("seg", "blk", None, None, None),
        P("seg", "blk", None),
        P("blk", None),
        P(None, ("groups", "seg"), None, "blk", None),
    )
    out_specs = (P(("groups", "seg"), None, "blk", None), P("groups"))
    body = functools.partial(on_device, mesh.shape["seg"], mesh.shape["blk"])
    return jax.shard_map(body, mesh=mesh, in_specs=in_specs, out_specs=out_specs, check_vma=False)
```

```python
import functools

import jax
import jax.numpy as jnp
from jax import lax
from jax.experimental import pallas as pl
from jax.experimental.pallas import tpu as pltpu
from jax.sharding import PartitionSpec as P

STEPS = 18
SWITCH = 5
MESH = pl.DeviceIdType.MESH
REACH = 2
PAD = 32
BATCH = 4
BORDER = (((0, 0), (1, 0), (1, 1)), ((0, 0), (0, 1), (1, 1)))


def merge_pair(total, first, stored, row, cols_at, tile_at, wet, accs, put):
    wide = 2 * REACH + 1
    for acc in accs:
        acc[...] = jnp.zeros_like(acc)

    def add(k, unused):
        for j in range(2):
            col = cols_at(row + j, k)
            d = lax.rem(col - first - row - j + (REACH + total), total)
            accs[j][d] += tile_at(j, k).astype(jnp.float32)
        return unused

    lax.fori_loop(0, stored, add, 0, unroll=4)
    size = accs[0].shape[1]
    for j in range(2):
        mask = wet(row + j).astype(jnp.float32)
        for c in range(wide + 1):
            d = c - j
            if 0 <= d < wide:
                put(c, j, (accs[j][d].T * mask).astype(jnp.bfloat16))
            else:
                put(c, j, jnp.zeros((size, size), jnp.bfloat16))


def merge_pairs(total, rows, groups, cols, wet_v, tile_buf, waits, accs, w_ref, then=None):
    first = lax.axis_index("blk") * rows
    segs = cols.shape[0]
    size = accs[0].shape[1]
    for i, g in enumerate(groups):
        for s in range(segs):
            for x in waits[i * segs + s]:
                x.wait()

            def put(c, j, part):
                w_ref[s, i, c * size:(c + 1) * size, j * size:(j + 1) * size] = part

            merge_pair(
                total, first, cols.shape[2], 2 * g, lambda row, k: cols[s, row, k],
                lambda j, k: tile_buf[s, 2 * i + j, k],
                lambda row: wet_v[pl.ds(row, 1), :], accs, put,
            )
            if then is not None:
                then(i, s)


def start_fetches(groups, cols_ref, wet_ref, tiles_ref, cols, wet_v, tile_buf, small_sem, tile_sem):
    small = [
        pltpu.make_async_copy(cols_ref, cols, small_sem.at[0]),
        pltpu.make_async_copy(wet_ref, wet_v, small_sem.at[1]),
    ]
    waits = []
    for i, g in enumerate(groups):
        for s in range(cols_ref.shape[0]):
            waits.append(
                [
                    pltpu.make_async_copy(
                        tiles_ref.at[s, 2 * g + j], tile_buf.at[s, 2 * i + j], tile_sem.at[s, 2 * i + j]
                    )
                    for j in range(2)
                ]
            )
    for x in small:
        x.start()
    for both in waits:
        for x in both:
            x.start()
    return small, waits


def mix_of(coup_ref, cc):
    tracers = coup_ref.shape[0]
    c = 0.5 * coup_ref[...]
    high = c.astype(jnp.bfloat16)
    low = (c - high.astype(jnp.float32)).astype(jnp.bfloat16)
    cc[...] = jnp.zeros_like(cc)
    cc[:tracers, 0:tracers] = high.astype(jnp.float32)
    cc[:tracers, PAD:PAD + tracers] = low.astype(jnp.float32)
    one = cc[...]
    blank = jnp.zeros_like(one)
    return jnp.concatenate(
        [
            jnp.concatenate([one if i == j else blank for j in range(BATCH)], axis=1)
            for i in range(BATCH)
        ],
        axis=0,
    ).astype(jnp.bfloat16)


def dot(a, b):
    return jnp.dot(a, b, preferred_element_type=jnp.float32)


def forced(mix, us, ks):
    out = []
    for i in range(0, len(us), BATCH):
        group = us[i:i + BATCH]
        n = len(group)
        xs = [(k * u).astype(jnp.bfloat16) for u, k in zip(group, ks[i:i + BATCH])]
        stack = jnp.concatenate([x for x in xs for unused in range(2)], axis=0)
        added = dot(mix[:n * PAD, :2 * n * PAD], stack)
        out += [(u + added[j * PAD:(j + 1) * PAD]).astype(jnp.bfloat16) for j, u in enumerate(group)]
    return out


def edge_kernel(
    dims, base_hbm, dir_hbm, coup_hbm, cols_ref, wet_ref, tiles_ref, w_ref, slope_ref, drive_ref, left_ref, right_ref,
    cols, wet_v, tile_buf, acc0, acc1, cc, base, direction, coup, w_v, slope_v, drive_v, out_v,
    small_sem, tile_sem, in_sem, w_sem, out_sem,
):
    segs, tracers, rows, points, total = dims
    pairs = rows // 2
    per = tracers * rows
    pair = 2 * points
    edges = (0, pairs - 1)
    fetches = [
        pltpu.make_async_copy(a, b, in_sem.at[i])
        for i, (a, b) in enumerate([(base_hbm, base), (dir_hbm, direction), (coup_hbm, coup)])
    ]
    for x in fetches:
        x.start()
    small, waits = start_fetches(edges, cols_ref, wet_ref, tiles_ref, cols, wet_v, tile_buf, small_sem, tile_sem)
    for x in fetches:
        x.wait()
    mix = mix_of(coup, cc)

    def native(ref, s, g):
        halves = [
            jnp.concatenate(
                [
                    ref[pl.ds(s * per + 2 * g + j, tracers, stride=rows), :],
                    jnp.zeros((PAD - tracers, points), jnp.float32),
                ],
                axis=0,
            )
            for j in range(2)
        ]
        return jnp.concatenate(halves, axis=1)

    units = [(s, g) for s in range(segs) for g in range(pairs)]
    slopes, starts = [], []
    for s, g in units:
        t = jnp.tanh(native(base, s, g))
        k = 1.0 - t * t
        slope_v[s, :, g * pair:(g + 1) * pair] = k
        slopes.append(k)
        starts.append(native(direction, s, g))
    drives = forced(mix, starts, slopes)
    for (s, g), d, k in zip(units, drives, slopes):
        drive_v[s, :, g * pair:(g + 1) * pair] = d
        if g in edges:
            high = k.astype(jnp.bfloat16)
            for i, x in enumerate((d, high)):
                for j in range(2):
                    at = 3 * points + (2 * i + j) * PAD
                    out_v[edges.index(g), s, at:at + PAD, :] = x[:, j * points:(j + 1) * points]
    for x in small:
        x.wait()
    outs = [
        pltpu.make_async_copy(slope_v, slope_ref, out_sem.at[0]),
        pltpu.make_async_copy(drive_v, drive_ref, out_sem.at[1]),
    ]
    for x in outs:
        x.start()

    def merged(i, s):
        for n, (c, j) in enumerate(BORDER[i]):
            c = c + i * 2 * REACH
            out_v[i, s, n * points:(n + 1) * points, :] = (
                w_v[s, i, c * points:(c + 1) * points, j * points:(j + 1) * points]
            )
        copy = pltpu.make_async_copy(w_v.at[s, i], w_ref.at[s, i], w_sem.at[s, i])
        copy.start()
        outs.append(copy)
        if s == segs - 1:
            copy = pltpu.make_async_copy(out_v.at[i], (left_ref, right_ref)[i], out_sem.at[2 + i])
            copy.start()
            outs.append(copy)

    merge_pairs(total, rows, edges, cols, wet_v, tile_buf, waits, (acc0, acc1), w_v, merged)
    for x in outs:
        x.wait()


def inner_kernel(
    dims, basis, cols_ref, wet_ref, tiles_ref, w_ref, gram_ref,
    cols, wet_v, tile_buf, acc0, acc1, small_sem, tile_sem,
):
    segs, tracers, rows, points, total = dims
    pairs = rows // 2
    kry = basis.shape[0]
    groups = tuple(range(1, pairs - 1))
    small, waits = start_fetches(groups, cols_ref, wet_ref, tiles_ref, cols, wet_v, tile_buf, small_sem, tile_sem)
    half = kry // 2 + 1

    def gram(i, acc):
        b = [basis[j, pl.ds(pl.multiple_of(i * rows, rows), rows), :] for j in range(kry)]
        return tuple(acc[m * kry + j] + b[j] * b[(j + m) % kry] for m in range(half) for j in range(kry))

    zero = jnp.zeros((rows, points), jnp.float32)
    sums = lax.fori_loop(0, segs * tracers, gram, (zero,) * (half * kry))
    for m in range(half):
        for j in range(kry):
            gram_ref[pl.ds(m * 8 + j, 1), :] = jnp.sum(sums[m * kry + j], axis=0, keepdims=True)
    for x in small:
        x.wait()
    merge_pairs(total, rows, groups, cols, wet_v, tile_buf, waits, (acc0, acc1), w_ref)


def steps_kernel(
    dims, slope, start, dir_ref, coup_ref, w_edge, w_inner, from_left, from_right, gram_in, basis, orth_ref, coef_ref,
    drive0, drive1, cc, follow, shalo, whalo, whalo2, hold, sent, came, part1, part2, gram1, gram2,
    send_sem, recv_sem, border_send, border_recv, follow_sem, red_sem1, red_sem2, gram_sem1, gram_sem2,
):
    segs, tracers, rows, points, kry, n_seg, n_blk, entries = dims
    pairs = rows // 2
    per = tracers * rows
    pair = 2 * points
    drive = (drive0, drive1)
    me_seg, me_blk = lax.axis_index("seg"), lax.axis_index("blk")
    left, right = lax.rem(me_blk + n_blk - 1, n_blk), lax.rem(me_blk + 1, n_blk)

    barrier = pltpu.get_barrier_semaphore()
    for i in range(1, n_blk):
        pl.semaphore_signal(barrier, inc=1, device_id={"blk": lax.rem(me_blk + i, n_blk)}, device_id_type=MESH)
    for i in range(1, n_seg):
        pl.semaphore_signal(barrier, inc=1, device_id={"seg": lax.rem(me_seg + i, n_seg)}, device_id_type=MESH)

    def lanes_of(g, count=1):
        return slice((g + 1) * pair, (g + 1 + count) * pair)

    mix = mix_of(coup_ref, cc)
    halos_in = (from_left, from_right)

    def force_into(units, to):
        values = forced(mix, [u for u, k, s, g in units], [k for u, k, s, g in units])
        for (u, k, s, g), v in zip(units, values):
            to[s, :, lanes_of(g)] = v

    def slope_of(s, g):
        return slope[s, :, g * pair:(g + 1) * pair]

    def beyond(s, side, i):
        at = 3 * points + 2 * i * PAD
        ref = halos_in[side]
        return jnp.concatenate([ref[s, at:at + PAD, :], ref[s, at + PAD:at + 2 * PAD, :]], axis=1)

    def slope_beyond(s, side):
        return shalo[side, s]

    edges = (0, pairs - 1)
    inner = range(1, pairs - 1)
    halo = (-1, pairs)
    for s in range(segs):
        drive0[s, :, pair:(pairs + 1) * pair] = start[s]
        for side in range(2):
            drive0[s, :, lanes_of(halo[side])] = beyond(s, side, 0)
            shalo[side, s] = beyond(s, side, 1).astype(jnp.float32)
            whalo[side, s] = jnp.zeros((pair, pair), jnp.bfloat16)
            for n, (c, j) in enumerate(BORDER[1 - side]):
                whalo[side, s, c * points:(c + 1) * points, j * points:(j + 1) * points] = (
                    halos_in[side][s, n * points:(n + 1) * points, :]
                )
    gram1[me_blk] = gram_in[...]
    follow_copy = pltpu.make_async_remote_copy(
        src_ref=dir_ref.at[0:per], dst_ref=follow, send_sem=follow_sem.at[0], recv_sem=follow_sem.at[1],
        device_id={"seg": lax.rem(me_seg + n_seg - 1, n_seg)}, device_id_type=MESH,
    )
    chunks = segs * tracers
    half = kry // 2 + 1

    def fold(a):
        return jnp.sum(a, axis=0, keepdims=True)

    def everyone(part, me, axis, count, sems):
        return [
            pltpu.make_async_remote_copy(
                src_ref=part.at[me], dst_ref=part.at[me],
                send_sem=sems.at[0, i - 1], recv_sem=sems.at[1, i - 1],
                device_id={axis: lax.rem(me + i, count)}, device_id_type=MESH,
            )
            for i in range(1, count)
        ]

    def total_of(part, copies, count):
        for x in copies:
            x.wait()
        result = part[0]
        for i in range(1, count):
            result = result + part[i]
        return result

    zero = jnp.zeros((rows, points), jnp.float32)
    gram_copies1 = everyone(gram1, me_blk, "blk", n_blk, gram_sem1)

    def message(n, side):
        return pltpu.make_async_remote_copy(
            src_ref=sent.at[n, side], dst_ref=came.at[n, 1 - side],
            send_sem=send_sem.at[n, side], recv_sem=recv_sem.at[n, 1 - side],
            device_id={"blk": (left, right)[side]}, device_id_type=MESH,
        )

    def arrival(n, side):
        return pltpu.make_async_remote_copy(
            src_ref=sent.at[n, 1 - side], dst_ref=came.at[n, side],
            send_sem=send_sem.at[n, 1 - side], recv_sem=recv_sem.at[n, side],
            device_id={"blk": (left, right)[1 - side]}, device_id_type=MESH,
        )

    def step(n, slot, halos, pieces):
        here, there = drive[slot], drive[1 - slot]
        own = [[None, None] for s in range(segs)]
        for s in range(segs):
            own[s][0] = dot(here[s, :, lanes_of(0, 2)], w_edge[s, 0, pair:3 * pair, :])
            own[s][1] = dot(here[s, :, lanes_of(pairs - 2, 2)], w_edge[s, 1, 0:2 * pair, :])
        def send():
            for side in range(2):
                for s in range(segs):
                    sent[n, side, s] = own[s][side].astype(jnp.bfloat16)
            if not halos:
                pl.semaphore_wait(barrier, n_blk + n_seg - 2)
            for side in range(2):
                message(n, side).start()
            for x in pieces:
                x.start()

        if halos:
            send()
        moved = {}
        for s in range(segs):
            for g in range(1, pairs - 1):
                moved[s, g] = dot(here[s, :, lanes_of(g - 1, 3)], w_inner[s, g - 1])
        if halos:
            mine = [
                [dot(there[s, :, lanes_of(edges[side])], whalo[side, s]) for side in range(2)]
                for s in range(segs)
            ]
        force_into([(moved[s, g], slope_of(s, g), s, g) for s in range(segs) for g in inner], there)
        if not halos:
            send()
        if halos:
            for side in range(2):
                arrival(n - 1, side).wait()
            force_into(
                [
                    (mine[s][side] + came[n - 1, side, s].astype(jnp.float32), slope_beyond(s, side), s, halo[side])
                    for s in range(segs)
                    for side in range(2)
                ],
                here,
            )
        for side in range(2):
            g = edges[side]
            for s in range(segs):
                moved[s, g] = own[s][side] + dot(
                    here[s, :, lanes_of(halo[side])], w_edge[s, side, side * 2 * pair:(side * 2 + 1) * pair, :]
                )
        force_into([(moved[s, g], slope_of(s, g), s, g) for s in range(segs) for g in edges], there)

    def beside(n, slot):
        here = drive[slot]
        for s in range(segs):
            r = (
                dot(here[s, :, lanes_of(1)], w_edge[s, 0, 2 * pair:3 * pair, :]),
                dot(here[s, :, lanes_of(pairs - 2)], w_edge[s, 1, 0:pair, :]),
            )
            for side in range(2):
                hold[slot, s, side] = r[side]
                sent[n, side, s] = r[side].astype(jnp.bfloat16)
        for side in range(2):
            message(n, side).start()

    def late_step(n, slot, finish):
        here, there = drive[slot], drive[1 - slot]
        moved = {}
        for s in range(segs):
            for g in inner:
                moved[s, g] = dot(here[s, :, lanes_of(g - 1, 3)], w_inner[s, g - 1])
        mine = {}
        for s in range(segs):
            for side in range(2):
                old = dot(there[s, :, lanes_of(halo[side])], whalo2[side, s])
                mine[s, side] = (
                    dot(there[s, :, lanes_of(edges[side])], whalo[side, s]) + jnp.where(n > SWITCH, old, 0.0)
                )
        if not finish:
            force_into([(moved[s, g], slope_of(s, g), s, g) for s in range(segs) for g in inner], there)
            beside(n + 1, 1 - slot)
        for side in range(2):
            arrival(n - 1, side).wait()
        force_into(
            [
                (mine[s, side] + came[n - 1, side, s].astype(jnp.float32), slope_beyond(s, side), s, halo[side])
                for s in range(segs)
                for side in range(2)
            ],
            here,
        )
        for side in range(2):
            g = edges[side]
            for s in range(segs):
                moved[s, g] = hold[slot, s, side] + dot(
                    here[s, :, lanes_of((-1, pairs - 1)[side], 2)], w_edge[s, side, side * pair:(side + 2) * pair, :]
                )
        if finish:
            for s in range(segs):
                for g in range(pairs):
                    for j in range(2):
                        orth_ref[pl.ds(s * per + 2 * g + j, tracers, stride=rows), :] = (
                            moved[s, g][:tracers, j * points:(j + 1) * points]
                        )
        else:
            force_into([(moved[s, g], slope_of(s, g), s, g) for s in range(segs) for g in edges], there)

    count = (SWITCH - 1) // segs
    size = pair // count
    borders = [
        [
            pltpu.make_async_remote_copy(
                src_ref=w_edge.at[s, side, pair + k * size:pair + (k + 1) * size, :],
                dst_ref=whalo2.at[1 - side, s, k * size:(k + 1) * size, :],
                send_sem=border_send.at[s * count + k, side], recv_sem=border_recv.at[s * count + k, side],
                device_id={"blk": (left, right)[side]}, device_id_type=MESH,
            )
            for side in range(2)
        ]
        for s in range(segs)
        for k in range(count)
    ]
    for n in range(SWITCH):
        step(n, n % 2, n > 0, borders[n] if n < len(borders) else [])
    follow_copy.start()
    for x in gram_copies1:
        x.start()
    beside(SWITCH, 1)
    for both in borders:
        for x in both:
            x.wait()

    def two_late(i, unused):
        late_step(SWITCH + 2 * i, 1, False)
        late_step(SWITCH + 2 * i + 1, 0, False)
        return unused

    lax.fori_loop(0, (STEPS - 1 - SWITCH) // 2, two_late, 0)
    late_step(STEPS - 1, 1, True)

    gram2[me_seg] = total_of(gram1, gram_copies1, n_blk)
    gram_copies2 = everyone(gram2, me_seg, "seg", n_seg, gram_sem2)
    for x in gram_copies2:
        x.start()
    follow_copy.wait()

    def project(i, acc):
        here = pl.ds(pl.multiple_of(i * rows, rows), rows)
        for s in range(segs):
            at = pl.ds(pl.multiple_of(i * rows, rows) + s * per, rows)
            if s < segs - 1:
                nxt = dir_ref[pl.ds(pl.multiple_of(i * rows, rows) + (s + 1) * per, rows), :]
            else:
                nxt = follow[here, :]
            shot = orth_ref[at, :] - nxt
            orth_ref[at, :] = shot
            acc = tuple(acc[j] + basis[j, at, :] * shot for j in range(kry)) + (acc[kry] + shot * shot,)
        return acc

    sums = lax.fori_loop(0, tracers, project, (zero,) * (kry + 1), unroll=4)
    for j in range(kry):
        part1[me_blk, pl.ds(j, 1), :] = fold(sums[j])
    part1[me_blk, pl.ds(8, 8), :] = sums[kry]

    copies = everyone(part1, me_blk, "blk", n_blk, red_sem1)
    for x in copies:
        x.start()
    for side in range(2):
        arrival(STEPS - 1, side).wait()
    part2[me_seg] = total_of(part1, copies, n_blk)
    copies = everyone(part2, me_seg, "seg", n_seg, red_sem2)
    for x in copies:
        x.start()
    gramd = jnp.sum(total_of(gram2, gram_copies2, n_seg), axis=1, keepdims=True)
    sumd = jnp.sum(total_of(part2, copies, n_seg), axis=1, keepdims=True)
    h = sumd[0:kry]
    hv = [sumd[j:j + 1] for j in range(kry)]
    quad = jnp.zeros((kry, 1), jnp.float32)
    for m in range(half):
        turned = h if m == 0 else jnp.concatenate([h[m:], h[:m]], axis=0)
        weight = 1.0 if m == 0 or 2 * m == kry else 2.0
        quad = quad + weight * (turned * gramd[m * 8:m * 8 + kry])
    quad = h * (quad - 2.0 * h) + sumd[8:16]
    square = jnp.sum(jnp.broadcast_to(quad, (kry, points)), axis=0, keepdims=True)
    length = jnp.sqrt(jnp.maximum(square, 0.0) / entries)
    coef_ref[kry] = length[0, 0]
    for j in range(kry):
        coef_ref[j] = hv[j][0, 0]
    wide = [jnp.broadcast_to(x, (rows, points)) for x in hv]

    def subtract(i, unused):
        at = pl.ds(pl.multiple_of(i * rows, rows), rows)
        a = hv_sum([wide[j] * basis[j, at, :] for j in range(kry)])
        orth_ref[at, :] = orth_ref[at, :] - a
        return unused

    lax.fori_loop(0, chunks, subtract, 0, unroll=4)


def hv_sum(terms):
    while len(terms) > 1:
        terms = [sum(terms[i:i + 2]) for i in range(0, len(terms), 2)]
    return terms[0]


def on_device(n_seg, n_blk, base_state, direction, coupling, tiles, columns, wet, basis):
    segs, tracers, rows, points = direction.shape
    stored = tiles.shape[2]
    kry = basis.shape[0]
    total = rows * n_blk
    entries = float(segs * n_seg * tracers * total * points)
    pairs = rows // 2
    pair = 2 * points
    wide = 2 * REACH + 2
    flat = segs * tracers * rows
    base_flat = base_state.reshape(flat, points)
    dir_flat = direction.reshape(flat, points)
    basis_flat = basis.reshape(kry, flat, points)
    in_vmem = pl.BlockSpec(memory_space=pltpu.VMEM)
    in_hbm = pl.BlockSpec(memory_space=pltpu.HBM)
    bf16, f32 = jnp.bfloat16, jnp.float32
    shape = jax.ShapeDtypeStruct

    def scratch_of(count):
        return [
            pltpu.SMEM((segs, rows, stored), jnp.int32),
            pltpu.VMEM((rows, points), jnp.int32),
            pltpu.VMEM((segs, 2 * count, stored, points, points), bf16),
            pltpu.VMEM((2 * REACH + 1, points, points), f32),
            pltpu.VMEM((2 * REACH + 1, points, points), f32),
        ]

    def sems_of(count):
        return [pltpu.SemaphoreType.DMA((2,)), pltpu.SemaphoreType.DMA((segs, 2 * count))]

    dims = (segs, tracers, rows, points, total)
    work = segs * rows * stored * points * points
    border = shape((segs, 3 * points + 4 * PAD, points), bf16)
    w_edge, slope, start, to_left, to_right = pl.pallas_call(
        functools.partial(edge_kernel, dims),
        out_shape=(
            shape((segs, 2, wide * points, pair), bf16), shape((segs, PAD, rows * points), f32),
            shape((segs, PAD, rows * points), bf16), border, border,
        ),
        in_specs=[in_hbm] * 6,
        out_specs=(in_hbm,) * 5,
        scratch_shapes=scratch_of(2) + [
            pltpu.VMEM((PAD, 2 * PAD), f32),
            pltpu.VMEM((flat, points), f32),
            pltpu.VMEM((flat, points), f32),
            pltpu.VMEM((tracers, tracers), f32),
            pltpu.VMEM((segs, 2, wide * points, pair), bf16),
            pltpu.VMEM((segs, PAD, rows * points), f32),
            pltpu.VMEM((segs, PAD, rows * points), bf16),
            pltpu.VMEM((2, segs, 3 * points + 4 * PAD, points), bf16),
        ] + sems_of(2) + [
            pltpu.SemaphoreType.DMA((3,)),
            pltpu.SemaphoreType.DMA((segs, 2)),
            pltpu.SemaphoreType.DMA((4,)),
        ],
        compiler_params=pltpu.CompilerParams(vmem_limit_bytes=56 << 20),
        cost_estimate=pl.CostEstimate(flops=8 * work, bytes_accessed=work, transcendentals=0),
        name="edge",
    )(base_flat, dir_flat, coupling, columns, wet, tiles)
    ring = range(n_blk)
    from_right = lax.ppermute(to_left, "blk", [(i, (i + n_blk - 1) % n_blk) for i in ring])
    from_left = lax.ppermute(to_right, "blk", [(i, (i + 1) % n_blk) for i in ring])
    w_inner, gram = pl.pallas_call(
        functools.partial(inner_kernel, dims),
        out_shape=(
            shape((segs, pairs - 2, wide * points, pair), bf16), shape(((kry // 2 + 1) * 8, points), f32),
        ),
        in_specs=[in_vmem] + [in_hbm] * 3,
        out_specs=(in_vmem,) * 2,
        scratch_shapes=scratch_of(pairs - 2) + sems_of(pairs - 2),
        compiler_params=pltpu.CompilerParams(vmem_limit_bytes=48 << 20),
        cost_estimate=pl.CostEstimate(flops=8 * work, bytes_accessed=work, transcendentals=0),
        name="inner",
    )(basis_flat, columns, wet, tiles)
    dims = (segs, tracers, rows, points, kry, n_seg, n_blk, entries)
    half = (kry // 2 + 1) * 8
    orth, coef = pl.pallas_call(
        functools.partial(steps_kernel, dims),
        out_shape=(
            jax.ShapeDtypeStruct((flat, points), jnp.float32),
            jax.ShapeDtypeStruct((kry + 1,), jnp.float32),
        ),
        in_specs=[in_vmem] * 10,
        out_specs=(in_vmem, pl.BlockSpec(memory_space=pltpu.SMEM)),
        scratch_shapes=[
            pltpu.VMEM((segs, PAD, (pairs + 2) * pair), jnp.bfloat16),
            pltpu.VMEM((segs, PAD, (pairs + 2) * pair), jnp.bfloat16),
            pltpu.VMEM((PAD, 2 * PAD), jnp.float32),
            pltpu.VMEM((tracers * rows, points), jnp.float32),
            pltpu.VMEM((2, segs, PAD, pair), jnp.float32),
            pltpu.VMEM((2, segs, pair, pair), jnp.bfloat16),
            pltpu.VMEM((2, segs, pair, pair), jnp.bfloat16),
            pltpu.VMEM((2, segs, 2, PAD, pair), jnp.float32),
            pltpu.VMEM((STEPS, 2, segs, PAD, pair), jnp.bfloat16),
            pltpu.VMEM((STEPS, 2, segs, PAD, pair), jnp.bfloat16),
            pltpu.VMEM((n_blk, 16, points), jnp.float32),
            pltpu.VMEM((n_seg, 16, points), jnp.float32),
            pltpu.VMEM((n_blk, half, points), jnp.float32),
            pltpu.VMEM((n_seg, half, points), jnp.float32),
            pltpu.SemaphoreType.DMA((STEPS, 2)),
            pltpu.SemaphoreType.DMA((STEPS, 2)),
            pltpu.SemaphoreType.DMA((SWITCH - 1, 2)),
            pltpu.SemaphoreType.DMA((SWITCH - 1, 2)),
            pltpu.SemaphoreType.DMA((2,)),
            pltpu.SemaphoreType.DMA((2, n_blk - 1)),
            pltpu.SemaphoreType.DMA((2, n_seg - 1)),
            pltpu.SemaphoreType.DMA((2, n_blk - 1)),
            pltpu.SemaphoreType.DMA((2, n_seg - 1)),
        ],
        compiler_params=pltpu.CompilerParams(
            collective_id=0, has_side_effects=True, vmem_limit_bytes=40 << 20
        ),
        name="steps",
    )(slope, start, dir_flat, coupling, w_edge, w_inner, from_left, from_right, gram, basis_flat)
    return orth.reshape(direction.shape), coef


def solution(mesh):
    in_specs = (
        P(("groups", "seg"), None, "blk", None),
        P(("groups", "seg"), None, "blk", None),
        P("groups", None),
        P("seg", "blk", None, None, None),
        P("seg", "blk", None),
        P("blk", None),
        P(None, ("groups", "seg"), None, "blk", None),
    )
    out_specs = (P(("groups", "seg"), None, "blk", None), P("groups"))
    body = functools.partial(on_device, mesh.shape["seg"], mesh.shape["blk"])
    return jax.shard_map(body, mesh=mesh, in_specs=in_specs, out_specs=out_specs, check_vma=False)
```

```python
import functools

import jax
import jax.numpy as jnp
from jax import lax
from jax.experimental import pallas as pl
from jax.experimental.pallas import tpu as pltpu
from jax.sharding import PartitionSpec as P

STEPS = 18
SWITCH = 5
MESH = pl.DeviceIdType.MESH
REACH = 2
PAD = 32
BATCH = 4
BORDER = (((0, 0), (1, 0), (1, 1)), ((0, 0), (0, 1), (1, 1)))


def merge_pair(total, first, stored, row, cols_at, tile_at, wet, accs, put):
    wide = 2 * REACH + 1
    for acc in accs:
        acc[...] = jnp.zeros_like(acc)

    def add(k, unused):
        for j in range(2):
            col = cols_at(row + j, k)
            d = lax.rem(col - first - row - j + (REACH + total), total)
            accs[j][d] += tile_at(j, k).astype(jnp.float32)
        return unused

    lax.fori_loop(0, stored, add, 0, unroll=8)
    size = accs[0].shape[1]
    for j in range(2):
        mask = wet(row + j).astype(jnp.float32).astype(jnp.bfloat16)
        for c in range(wide + 1):
            d = c - j
            if 0 <= d < wide:
                put(c, j, accs[j][d].astype(jnp.bfloat16).T * mask)
            else:
                put(c, j, jnp.zeros((size, size), jnp.bfloat16))


def merge_pairs(total, rows, groups, cols, wet_v, tile_buf, waits, accs, w_ref, then=None):
    first = lax.axis_index("blk") * rows
    segs = cols.shape[0]
    size = accs[0].shape[1]
    for i, g in enumerate(groups):
        for s in range(segs):
            for x in waits[i * segs + s]:
                x.wait()

            def put(c, j, part):
                w_ref[s, i, c * size:(c + 1) * size, j * size:(j + 1) * size] = part

            merge_pair(
                total, first, cols.shape[2], 2 * g, lambda row, k: cols[s, row, k],
                lambda j, k: tile_buf[s, 2 * i + j, k],
                lambda row: wet_v[pl.ds(row, 1), :], accs, put,
            )
            if then is not None:
                then(i, s)


def start_fetches(groups, cols_ref, wet_ref, tiles_ref, cols, wet_v, tile_buf, small_sem, tile_sem):
    small = [
        pltpu.make_async_copy(cols_ref, cols, small_sem.at[0]),
        pltpu.make_async_copy(wet_ref, wet_v, small_sem.at[1]),
    ]
    waits = []
    for i, g in enumerate(groups):
        for s in range(cols_ref.shape[0]):
            waits.append(
                [
                    pltpu.make_async_copy(
                        tiles_ref.at[s, 2 * g + j], tile_buf.at[s, 2 * i + j], tile_sem.at[s, 2 * i + j]
                    )
                    for j in range(2)
                ]
            )
    for x in small:
        x.start()
    for both in waits:
        for x in both:
            x.start()
    return small, waits


def mix_of(coup_ref, cc):
    tracers = coup_ref.shape[0]
    c = 0.5 * coup_ref[...]
    high = c.astype(jnp.bfloat16)
    low = (c - high.astype(jnp.float32)).astype(jnp.bfloat16)
    cc[...] = jnp.zeros_like(cc)
    cc[:tracers, 0:tracers] = high.astype(jnp.float32)
    cc[:tracers, PAD:PAD + tracers] = low.astype(jnp.float32)
    one = cc[...]
    blank = jnp.zeros_like(one)
    return jnp.concatenate(
        [
            jnp.concatenate([one if i == j else blank for j in range(BATCH)], axis=1)
            for i in range(BATCH)
        ],
        axis=0,
    ).astype(jnp.bfloat16)


def dot(a, b):
    return jnp.dot(a, b, preferred_element_type=jnp.float32)


def forced(mix, us, ks):
    out = []
    for i in range(0, len(us), BATCH):
        group = us[i:i + BATCH]
        n = len(group)
        xs = [(k * u).astype(jnp.bfloat16) for u, k in zip(group, ks[i:i + BATCH])]
        stack = jnp.concatenate([x for x in xs for unused in range(2)], axis=0)
        added = dot(mix[:n * PAD, :2 * n * PAD], stack)
        out += [(u + added[j * PAD:(j + 1) * PAD]).astype(jnp.bfloat16) for j, u in enumerate(group)]
    return out


def edge_kernel(
    dims, base_hbm, dir_hbm, coup_hbm, cols_ref, wet_ref, tiles_ref, w_ref, slope_ref, drive_ref, left_ref, right_ref,
    cols, wet_v, tile_buf, acc0, acc1, cc, base, direction, coup, w_v, slope_v, drive_v, out_v,
    small_sem, tile_sem, in_sem, w_sem, out_sem,
):
    segs, tracers, rows, points, total = dims
    pairs = rows // 2
    per = tracers * rows
    pair = 2 * points
    edges = (0, pairs - 1)
    fetches = [
        pltpu.make_async_copy(a, b, in_sem.at[i])
        for i, (a, b) in enumerate([(base_hbm, base), (dir_hbm, direction), (coup_hbm, coup)])
    ]
    for x in fetches:
        x.start()
    small, waits = start_fetches(edges, cols_ref, wet_ref, tiles_ref, cols, wet_v, tile_buf, small_sem, tile_sem)
    for x in fetches:
        x.wait()
    mix = mix_of(coup, cc)

    def native(ref, s, g):
        halves = [
            jnp.concatenate(
                [
                    ref[pl.ds(s * per + 2 * g + j, tracers, stride=rows), :],
                    jnp.zeros((PAD - tracers, points), jnp.float32),
                ],
                axis=0,
            )
            for j in range(2)
        ]
        return jnp.concatenate(halves, axis=1)

    units = [(s, g) for s in range(segs) for g in range(pairs)]
    slopes, starts = [], []
    for s, g in units:
        t = jnp.tanh(native(base, s, g))
        k = 1.0 - t * t
        slope_v[s, :, g * pair:(g + 1) * pair] = k
        slopes.append(k)
        starts.append(native(direction, s, g))
    drives = forced(mix, starts, slopes)
    for (s, g), d, k in zip(units, drives, slopes):
        drive_v[s, :, g * pair:(g + 1) * pair] = d
        if g in edges:
            high = k.astype(jnp.bfloat16)
            for i, x in enumerate((d, high)):
                for j in range(2):
                    at = 3 * points + (2 * i + j) * PAD
                    out_v[edges.index(g), s, at:at + PAD, :] = x[:, j * points:(j + 1) * points]
    for x in small:
        x.wait()
    outs = [
        pltpu.make_async_copy(slope_v, slope_ref, out_sem.at[0]),
        pltpu.make_async_copy(drive_v, drive_ref, out_sem.at[1]),
    ]
    for x in outs:
        x.start()

    def merged(i, s):
        for n, (c, j) in enumerate(BORDER[i]):
            c = c + i * 2 * REACH
            out_v[i, s, n * points:(n + 1) * points, :] = (
                w_v[s, i, c * points:(c + 1) * points, j * points:(j + 1) * points]
            )
        copy = pltpu.make_async_copy(w_v.at[s, i], w_ref.at[s, i], w_sem.at[s, i])
        copy.start()
        outs.append(copy)
        if s == segs - 1:
            copy = pltpu.make_async_copy(out_v.at[i], (left_ref, right_ref)[i], out_sem.at[2 + i])
            copy.start()
            outs.append(copy)

    merge_pairs(total, rows, edges, cols, wet_v, tile_buf, waits, (acc0, acc1), w_v, merged)
    for x in outs:
        x.wait()


def inner_kernel(
    dims, basis, cols_ref, wet_ref, tiles_ref, w_ref, gram_ref,
    cols, wet_v, tile_buf, acc0, acc1, small_sem, tile_sem,
):
    segs, tracers, rows, points, total = dims
    pairs = rows // 2
    kry = basis.shape[0]
    groups = tuple(range(1, pairs - 1))
    small, waits = start_fetches(groups, cols_ref, wet_ref, tiles_ref, cols, wet_v, tile_buf, small_sem, tile_sem)
    half = kry // 2 + 1

    def gram(i, acc):
        b = [basis[j, pl.ds(pl.multiple_of(i * rows, rows), rows), :] for j in range(kry)]
        return tuple(acc[m * kry + j] + b[j] * b[(j + m) % kry] for m in range(half) for j in range(kry))

    zero = jnp.zeros((rows, points), jnp.float32)
    sums = lax.fori_loop(0, segs * tracers, gram, (zero,) * (half * kry))
    for m in range(half):
        for j in range(kry):
            gram_ref[pl.ds(m * 8 + j, 1), :] = jnp.sum(sums[m * kry + j], axis=0, keepdims=True)
    for x in small:
        x.wait()
    merge_pairs(total, rows, groups, cols, wet_v, tile_buf, waits, (acc0, acc1), w_ref)


def steps_kernel(
    dims, slope, start, dir_ref, coup_ref, w_edge, w_inner, from_left, from_right, gram_in, basis, orth_ref, coef_ref,
    drive0, drive1, cc, follow, shalo, whalo, whalo2, hold, sent, came, part1, part2, gram1, gram2,
    send_sem, recv_sem, border_send, border_recv, follow_sem, red_sem1, red_sem2, gram_sem1, gram_sem2,
):
    segs, tracers, rows, points, kry, n_seg, n_blk, entries = dims
    pairs = rows // 2
    per = tracers * rows
    pair = 2 * points
    drive = (drive0, drive1)
    me_seg, me_blk = lax.axis_index("seg"), lax.axis_index("blk")
    left, right = lax.rem(me_blk + n_blk - 1, n_blk), lax.rem(me_blk + 1, n_blk)

    barrier = pltpu.get_barrier_semaphore()
    for i in range(1, n_blk):
        pl.semaphore_signal(barrier, inc=1, device_id={"blk": lax.rem(me_blk + i, n_blk)}, device_id_type=MESH)
    for i in range(1, n_seg):
        pl.semaphore_signal(barrier, inc=1, device_id={"seg": lax.rem(me_seg + i, n_seg)}, device_id_type=MESH)

    def lanes_of(g, count=1):
        return slice((g + 1) * pair, (g + 1 + count) * pair)

    mix = mix_of(coup_ref, cc)
    halos_in = (from_left, from_right)

    def force_into(units, to):
        values = forced(mix, [u for u, k, s, g in units], [k for u, k, s, g in units])
        for (u, k, s, g), v in zip(units, values):
            to[s, :, lanes_of(g)] = v

    def slope_of(s, g):
        return slope[s, :, g * pair:(g + 1) * pair]

    def beyond(s, side, i):
        at = 3 * points + 2 * i * PAD
        ref = halos_in[side]
        return jnp.concatenate([ref[s, at:at + PAD, :], ref[s, at + PAD:at + 2 * PAD, :]], axis=1)

    def slope_beyond(s, side):
        return shalo[side, s]

    edges = (0, pairs - 1)
    inner = range(1, pairs - 1)
    halo = (-1, pairs)
    for s in range(segs):
        drive0[s, :, pair:(pairs + 1) * pair] = start[s]
        for side in range(2):
            drive0[s, :, lanes_of(halo[side])] = beyond(s, side, 0)
            shalo[side, s] = beyond(s, side, 1).astype(jnp.float32)
            whalo[side, s] = jnp.zeros((pair, pair), jnp.bfloat16)
            for n, (c, j) in enumerate(BORDER[1 - side]):
                whalo[side, s, c * points:(c + 1) * points, j * points:(j + 1) * points] = (
                    halos_in[side][s, n * points:(n + 1) * points, :]
                )
    gram1[me_blk] = gram_in[...]
    follow_copy = pltpu.make_async_remote_copy(
        src_ref=dir_ref.at[0:per], dst_ref=follow, send_sem=follow_sem.at[0], recv_sem=follow_sem.at[1],
        device_id={"seg": lax.rem(me_seg + n_seg - 1, n_seg)}, device_id_type=MESH,
    )
    chunks = segs * tracers
    half = kry // 2 + 1

    def fold(a):
        return jnp.sum(a, axis=0, keepdims=True)

    def everyone(part, me, axis, count, sems):
        return [
            pltpu.make_async_remote_copy(
                src_ref=part.at[me], dst_ref=part.at[me],
                send_sem=sems.at[0, i - 1], recv_sem=sems.at[1, i - 1],
                device_id={axis: lax.rem(me + i, count)}, device_id_type=MESH,
            )
            for i in range(1, count)
        ]

    def total_of(part, copies, count):
        for x in copies:
            x.wait()
        result = part[0]
        for i in range(1, count):
            result = result + part[i]
        return result

    zero = jnp.zeros((rows, points), jnp.float32)
    gram_copies1 = everyone(gram1, me_blk, "blk", n_blk, gram_sem1)

    def message(n, side):
        return pltpu.make_async_remote_copy(
            src_ref=sent.at[n, side], dst_ref=came.at[n, 1 - side],
            send_sem=send_sem.at[n, side], recv_sem=recv_sem.at[n, 1 - side],
            device_id={"blk": (left, right)[side]}, device_id_type=MESH,
        )

    def arrival(n, side):
        return pltpu.make_async_remote_copy(
            src_ref=sent.at[n, 1 - side], dst_ref=came.at[n, side],
            send_sem=send_sem.at[n, 1 - side], recv_sem=recv_sem.at[n, side],
            device_id={"blk": (left, right)[1 - side]}, device_id_type=MESH,
        )

    def step(n, slot, halos, pieces):
        here, there = drive[slot], drive[1 - slot]
        own = [[None, None] for s in range(segs)]
        for s in range(segs):
            own[s][0] = dot(here[s, :, lanes_of(0, 2)], w_edge[s, 0, pair:3 * pair, :])
            own[s][1] = dot(here[s, :, lanes_of(pairs - 2, 2)], w_edge[s, 1, 0:2 * pair, :])
        def send():
            for side in range(2):
                for s in range(segs):
                    sent[n, side, s] = own[s][side].astype(jnp.bfloat16)
            if not halos:
                pl.semaphore_wait(barrier, n_blk + n_seg - 2)
            for side in range(2):
                message(n, side).start()
            for x in pieces:
                x.start()

        if halos:
            send()
        moved = {}
        for s in range(segs):
            for g in range(1, pairs - 1):
                moved[s, g] = dot(here[s, :, lanes_of(g - 1, 3)], w_inner[s, g - 1])
        if halos:
            mine = [
                [dot(there[s, :, lanes_of(edges[side])], whalo[side, s]) for side in range(2)]
                for s in range(segs)
            ]
        force_into([(moved[s, g], slope_of(s, g), s, g) for s in range(segs) for g in inner], there)
        if not halos:
            send()
        if halos:
            for side in range(2):
                arrival(n - 1, side).wait()
            force_into(
                [
                    (mine[s][side] + came[n - 1, side, s].astype(jnp.float32), slope_beyond(s, side), s, halo[side])
                    for s in range(segs)
                    for side in range(2)
                ],
                here,
            )
        for side in range(2):
            g = edges[side]
            for s in range(segs):
                moved[s, g] = own[s][side] + dot(
                    here[s, :, lanes_of(halo[side])], w_edge[s, side, side * 2 * pair:(side * 2 + 1) * pair, :]
                )
        force_into([(moved[s, g], slope_of(s, g), s, g) for s in range(segs) for g in edges], there)

    def beside(n, slot):
        here = drive[slot]
        for s in range(segs):
            r = (
                dot(here[s, :, lanes_of(1)], w_edge[s, 0, 2 * pair:3 * pair, :]),
                dot(here[s, :, lanes_of(pairs - 2)], w_edge[s, 1, 0:pair, :]),
            )
            for side in range(2):
                hold[slot, s, side] = r[side]
                sent[n, side, s] = r[side].astype(jnp.bfloat16)
        for side in range(2):
            message(n, side).start()

    def late_step(n, slot, finish):
        here, there = drive[slot], drive[1 - slot]
        moved = {}
        for s in range(segs):
            for g in inner:
                moved[s, g] = dot(here[s, :, lanes_of(g - 1, 3)], w_inner[s, g - 1])
        mine = {}
        for s in range(segs):
            for side in range(2):
                old = dot(there[s, :, lanes_of(halo[side])], whalo2[side, s])
                mine[s, side] = (
                    dot(there[s, :, lanes_of(edges[side])], whalo[side, s]) + jnp.where(n > SWITCH, old, 0.0)
                )
        if not finish:
            force_into([(moved[s, g], slope_of(s, g), s, g) for s in range(segs) for g in inner], there)
            beside(n + 1, 1 - slot)
        for side in range(2):
            arrival(n - 1, side).wait()
        force_into(
            [
                (mine[s, side] + came[n - 1, side, s].astype(jnp.float32), slope_beyond(s, side), s, halo[side])
                for s in range(segs)
                for side in range(2)
            ],
            here,
        )
        for side in range(2):
            g = edges[side]
            for s in range(segs):
                moved[s, g] = hold[slot, s, side] + dot(
                    here[s, :, lanes_of((-1, pairs - 1)[side], 2)], w_edge[s, side, side * pair:(side + 2) * pair, :]
                )
        if finish:
            for s in range(segs):
                for g in range(pairs):
                    for j in range(2):
                        orth_ref[pl.ds(s * per + 2 * g + j, tracers, stride=rows), :] = (
                            moved[s, g][:tracers, j * points:(j + 1) * points]
                        )
        else:
            force_into([(moved[s, g], slope_of(s, g), s, g) for s in range(segs) for g in edges], there)

    count = (SWITCH - 1) // segs
    size = pair // count
    borders = [
        [
            pltpu.make_async_remote_copy(
                src_ref=w_edge.at[s, side, pair + k * size:pair + (k + 1) * size, :],
                dst_ref=whalo2.at[1 - side, s, k * size:(k + 1) * size, :],
                send_sem=border_send.at[s * count + k, side], recv_sem=border_recv.at[s * count + k, side],
                device_id={"blk": (left, right)[side]}, device_id_type=MESH,
            )
            for side in range(2)
        ]
        for s in range(segs)
        for k in range(count)
    ]
    for n in range(SWITCH):
        step(n, n % 2, n > 0, borders[n] if n < len(borders) else [])
    follow_copy.start()
    for x in gram_copies1:
        x.start()
    beside(SWITCH, 1)
    for both in borders:
        for x in both:
            x.wait()

    def two_late(i, unused):
        late_step(SWITCH + 2 * i, 1, False)
        late_step(SWITCH + 2 * i + 1, 0, False)
        return unused

    lax.fori_loop(0, (STEPS - 1 - SWITCH) // 2, two_late, 0)
    late_step(STEPS - 1, 1, True)

    gram2[me_seg] = total_of(gram1, gram_copies1, n_blk)
    gram_copies2 = everyone(gram2, me_seg, "seg", n_seg, gram_sem2)
    for x in gram_copies2:
        x.start()
    follow_copy.wait()

    def project(i, acc):
        here = pl.ds(pl.multiple_of(i * rows, rows), rows)
        for s in range(segs):
            at = pl.ds(pl.multiple_of(i * rows, rows) + s * per, rows)
            if s < segs - 1:
                nxt = dir_ref[pl.ds(pl.multiple_of(i * rows, rows) + (s + 1) * per, rows), :]
            else:
                nxt = follow[here, :]
            shot = orth_ref[at, :] - nxt
            orth_ref[at, :] = shot
            acc = tuple(acc[j] + basis[j, at, :] * shot for j in range(kry)) + (acc[kry] + shot * shot,)
        return acc

    sums = lax.fori_loop(0, tracers, project, (zero,) * (kry + 1), unroll=4)
    for j in range(kry):
        part1[me_blk, pl.ds(j, 1), :] = fold(sums[j])
    part1[me_blk, pl.ds(8, 8), :] = sums[kry]

    copies = everyone(part1, me_blk, "blk", n_blk, red_sem1)
    for x in copies:
        x.start()
    for side in range(2):
        arrival(STEPS - 1, side).wait()
    part2[me_seg] = total_of(part1, copies, n_blk)
    copies = everyone(part2, me_seg, "seg", n_seg, red_sem2)
    for x in copies:
        x.start()
    gramd = jnp.sum(total_of(gram2, gram_copies2, n_seg), axis=1, keepdims=True)
    sumd = jnp.sum(total_of(part2, copies, n_seg), axis=1, keepdims=True)
    h = sumd[0:kry]
    hv = [sumd[j:j + 1] for j in range(kry)]
    quad = jnp.zeros((kry, 1), jnp.float32)
    for m in range(half):
        turned = h if m == 0 else jnp.concatenate([h[m:], h[:m]], axis=0)
        weight = 1.0 if m == 0 or 2 * m == kry else 2.0
        quad = quad + weight * (turned * gramd[m * 8:m * 8 + kry])
    quad = h * (quad - 2.0 * h) + sumd[8:16]
    square = jnp.sum(jnp.broadcast_to(quad, (kry, points)), axis=0, keepdims=True)
    length = jnp.sqrt(jnp.maximum(square, 0.0) / entries)
    coef_ref[kry] = length[0, 0]
    for j in range(kry):
        coef_ref[j] = hv[j][0, 0]
    wide = [jnp.broadcast_to(x, (rows, points)) for x in hv]

    def subtract(i, unused):
        at = pl.ds(pl.multiple_of(i * rows, rows), rows)
        a = hv_sum([wide[j] * basis[j, at, :] for j in range(kry)])
        orth_ref[at, :] = orth_ref[at, :] - a
        return unused

    lax.fori_loop(0, chunks, subtract, 0, unroll=4)


def hv_sum(terms):
    while len(terms) > 1:
        terms = [sum(terms[i:i + 2]) for i in range(0, len(terms), 2)]
    return terms[0]


def on_device(n_seg, n_blk, base_state, direction, coupling, tiles, columns, wet, basis):
    segs, tracers, rows, points = direction.shape
    stored = tiles.shape[2]
    kry = basis.shape[0]
    total = rows * n_blk
    entries = float(segs * n_seg * tracers * total * points)
    pairs = rows // 2
    pair = 2 * points
    wide = 2 * REACH + 2
    flat = segs * tracers * rows
    base_flat = base_state.reshape(flat, points)
    dir_flat = direction.reshape(flat, points)
    basis_flat = basis.reshape(kry, flat, points)
    in_vmem = pl.BlockSpec(memory_space=pltpu.VMEM)
    in_hbm = pl.BlockSpec(memory_space=pltpu.HBM)
    bf16, f32 = jnp.bfloat16, jnp.float32
    shape = jax.ShapeDtypeStruct

    def scratch_of(count):
        return [
            pltpu.SMEM((segs, rows, stored), jnp.int32),
            pltpu.VMEM((rows, points), jnp.int32),
            pltpu.VMEM((segs, 2 * count, stored, points, points), bf16),
            pltpu.VMEM((2 * REACH + 1, points, points), f32),
            pltpu.VMEM((2 * REACH + 1, points, points), f32),
        ]

    def sems_of(count):
        return [pltpu.SemaphoreType.DMA((2,)), pltpu.SemaphoreType.DMA((segs, 2 * count))]

    dims = (segs, tracers, rows, points, total)
    work = segs * rows * stored * points * points
    border = shape((segs, 3 * points + 4 * PAD, points), bf16)
    w_edge, slope, start, to_left, to_right = pl.pallas_call(
        functools.partial(edge_kernel, dims),
        out_shape=(
            shape((segs, 2, wide * points, pair), bf16), shape((segs, PAD, rows * points), f32),
            shape((segs, PAD, rows * points), bf16), border, border,
        ),
        in_specs=[in_hbm] * 6,
        out_specs=(in_hbm,) * 5,
        scratch_shapes=scratch_of(2) + [
            pltpu.VMEM((PAD, 2 * PAD), f32),
            pltpu.VMEM((flat, points), f32),
            pltpu.VMEM((flat, points), f32),
            pltpu.VMEM((tracers, tracers), f32),
            pltpu.VMEM((segs, 2, wide * points, pair), bf16),
            pltpu.VMEM((segs, PAD, rows * points), f32),
            pltpu.VMEM((segs, PAD, rows * points), bf16),
            pltpu.VMEM((2, segs, 3 * points + 4 * PAD, points), bf16),
        ] + sems_of(2) + [
            pltpu.SemaphoreType.DMA((3,)),
            pltpu.SemaphoreType.DMA((segs, 2)),
            pltpu.SemaphoreType.DMA((4,)),
        ],
        compiler_params=pltpu.CompilerParams(vmem_limit_bytes=56 << 20),
        cost_estimate=pl.CostEstimate(flops=8 * work, bytes_accessed=work, transcendentals=0),
        name="edge",
    )(base_flat, dir_flat, coupling, columns, wet, tiles)
    ring = range(n_blk)
    from_right = lax.ppermute(to_left, "blk", [(i, (i + n_blk - 1) % n_blk) for i in ring])
    from_left = lax.ppermute(to_right, "blk", [(i, (i + 1) % n_blk) for i in ring])
    w_inner, gram = pl.pallas_call(
        functools.partial(inner_kernel, dims),
        out_shape=(
            shape((segs, pairs - 2, wide * points, pair), bf16), shape(((kry // 2 + 1) * 8, points), f32),
        ),
        in_specs=[in_vmem] + [in_hbm] * 3,
        out_specs=(in_vmem,) * 2,
        scratch_shapes=scratch_of(pairs - 2) + sems_of(pairs - 2),
        compiler_params=pltpu.CompilerParams(vmem_limit_bytes=48 << 20),
        cost_estimate=pl.CostEstimate(flops=8 * work, bytes_accessed=work, transcendentals=0),
        name="inner",
    )(basis_flat, columns, wet, tiles)
    dims = (segs, tracers, rows, points, kry, n_seg, n_blk, entries)
    half = (kry // 2 + 1) * 8
    orth, coef = pl.pallas_call(
        functools.partial(steps_kernel, dims),
        out_shape=(
            jax.ShapeDtypeStruct((flat, points), jnp.float32),
            jax.ShapeDtypeStruct((kry + 1,), jnp.float32),
        ),
        in_specs=[in_vmem] * 10,
        out_specs=(in_vmem, pl.BlockSpec(memory_space=pltpu.SMEM)),
        scratch_shapes=[
            pltpu.VMEM((segs, PAD, (pairs + 2) * pair), jnp.bfloat16),
            pltpu.VMEM((segs, PAD, (pairs + 2) * pair), jnp.bfloat16),
            pltpu.VMEM((PAD, 2 * PAD), jnp.float32),
            pltpu.VMEM((tracers * rows, points), jnp.float32),
            pltpu.VMEM((2, segs, PAD, pair), jnp.float32),
            pltpu.VMEM((2, segs, pair, pair), jnp.bfloat16),
            pltpu.VMEM((2, segs, pair, pair), jnp.bfloat16),
            pltpu.VMEM((2, segs, 2, PAD, pair), jnp.float32),
            pltpu.VMEM((STEPS, 2, segs, PAD, pair), jnp.bfloat16),
            pltpu.VMEM((STEPS, 2, segs, PAD, pair), jnp.bfloat16),
            pltpu.VMEM((n_blk, 16, points), jnp.float32),
            pltpu.VMEM((n_seg, 16, points), jnp.float32),
            pltpu.VMEM((n_blk, half, points), jnp.float32),
            pltpu.VMEM((n_seg, half, points), jnp.float32),
            pltpu.SemaphoreType.DMA((STEPS, 2)),
            pltpu.SemaphoreType.DMA((STEPS, 2)),
            pltpu.SemaphoreType.DMA((SWITCH - 1, 2)),
            pltpu.SemaphoreType.DMA((SWITCH - 1, 2)),
            pltpu.SemaphoreType.DMA((2,)),
            pltpu.SemaphoreType.DMA((2, n_blk - 1)),
            pltpu.SemaphoreType.DMA((2, n_seg - 1)),
            pltpu.SemaphoreType.DMA((2, n_blk - 1)),
            pltpu.SemaphoreType.DMA((2, n_seg - 1)),
        ],
        compiler_params=pltpu.CompilerParams(
            collective_id=0, has_side_effects=True, vmem_limit_bytes=40 << 20
        ),
        name="steps",
    )(slope, start, dir_flat, coupling, w_edge, w_inner, from_left, from_right, gram, basis_flat)
    return orth.reshape(direction.shape), coef


def solution(mesh):
    in_specs = (
        P(("groups", "seg"), None, "blk", None),
        P(("groups", "seg"), None, "blk", None),
        P("groups", None),
        P("seg", "blk", None, None, None),
        P("seg", "blk", None),
        P("blk", None),
        P(None, ("groups", "seg"), None, "blk", None),
    )
    out_specs = (P(("groups", "seg"), None, "blk", None), P("groups"))
    body = functools.partial(on_device, mesh.shape["seg"], mesh.shape["blk"])
    return jax.shard_map(body, mesh=mesh, in_specs=in_specs, out_specs=out_specs, check_vma=False)
```

```python
import functools

import jax
import jax.numpy as jnp
from jax import lax
from jax.experimental import pallas as pl
from jax.experimental.pallas import tpu as pltpu
from jax.sharding import PartitionSpec as P

STEPS = 18
SWITCH = 5
MESH = pl.DeviceIdType.MESH
REACH = 2
PAD = 32
BATCH = 4
BORDER = (((0, 0), (1, 0), (1, 1)), ((0, 0), (0, 1), (1, 1)))


def merge_pair(total, first, stored, row, cols_at, tile_at, wet, accs, put):
    wide = 2 * REACH + 1
    for acc in accs:
        acc[...] = jnp.zeros_like(acc)

    def add(k, unused):
        for j in range(2):
            col = cols_at(row + j, k)
            d = lax.rem(col - first - row - j + (REACH + total), total)
            accs[j][d] += tile_at(j, k).astype(jnp.float32)
        return unused

    lax.fori_loop(0, stored, add, 0, unroll=8)
    size = accs[0].shape[1]
    for j in range(2):
        mask = wet(row + j).astype(jnp.float32).astype(jnp.bfloat16)
        for c in range(wide + 1):
            d = c - j
            if 0 <= d < wide:
                put(c, j, accs[j][d].astype(jnp.bfloat16).T * mask)
            else:
                put(c, j, jnp.zeros((size, size), jnp.bfloat16))


def merge_pairs(total, rows, groups, cols, wet_v, tile_buf, waits, accs, w_ref, then=None):
    first = lax.axis_index("blk") * rows
    segs = cols.shape[0]
    size = accs[0].shape[1]
    for i, g in enumerate(groups):
        for s in range(segs):
            for x in waits[i * segs + s]:
                x.wait()

            def put(c, j, part):
                w_ref[s, i, c * size:(c + 1) * size, j * size:(j + 1) * size] = part

            merge_pair(
                total, first, cols.shape[2], 2 * g, lambda row, k: cols[s, row, k],
                lambda j, k: tile_buf[s, 2 * i + j, k],
                lambda row: wet_v[pl.ds(row, 1), :], accs, put,
            )
            if then is not None:
                then(i, s)


def start_fetches(groups, cols_ref, wet_ref, tiles_ref, cols, wet_v, tile_buf, small_sem, tile_sem):
    small = [
        pltpu.make_async_copy(cols_ref, cols, small_sem.at[0]),
        pltpu.make_async_copy(wet_ref, wet_v, small_sem.at[1]),
    ]
    waits = []
    for i, g in enumerate(groups):
        for s in range(cols_ref.shape[0]):
            waits.append(
                [
                    pltpu.make_async_copy(
                        tiles_ref.at[s, 2 * g + j], tile_buf.at[s, 2 * i + j], tile_sem.at[s, 2 * i + j]
                    )
                    for j in range(2)
                ]
            )
    for x in small:
        x.start()
    for both in waits:
        for x in both:
            x.start()
    return small, waits


def mix_of(coup_ref, cc):
    tracers = coup_ref.shape[0]
    c = 0.5 * coup_ref[...]
    high = c.astype(jnp.bfloat16)
    low = (c - high.astype(jnp.float32)).astype(jnp.bfloat16)
    cc[...] = jnp.zeros_like(cc)
    cc[:tracers, 0:tracers] = high.astype(jnp.float32)
    cc[:tracers, PAD:PAD + tracers] = low.astype(jnp.float32)
    one = cc[...]
    blank = jnp.zeros_like(one)
    return jnp.concatenate(
        [
            jnp.concatenate([one if i == j else blank for j in range(BATCH)], axis=1)
            for i in range(BATCH)
        ],
        axis=0,
    ).astype(jnp.bfloat16)


def dot(a, b):
    return jnp.dot(a, b, preferred_element_type=jnp.float32)


def forced(mix, us, ks):
    out = []
    for i in range(0, len(us), BATCH):
        group = us[i:i + BATCH]
        n = len(group)
        xs = [(k * u).astype(jnp.bfloat16) for u, k in zip(group, ks[i:i + BATCH])]
        stack = jnp.concatenate([x for x in xs for unused in range(2)], axis=0)
        added = dot(mix[:n * PAD, :2 * n * PAD], stack)
        out += [(u + added[j * PAD:(j + 1) * PAD]).astype(jnp.bfloat16) for j, u in enumerate(group)]
    return out


def edge_kernel(
    dims, base_hbm, dir_hbm, coup_hbm, cols_ref, wet_ref, tiles_ref, w_ref, slope_ref, drive_ref, left_ref, right_ref,
    cols, wet_v, tile_buf, acc0, acc1, cc, base, direction, coup, w_v, slope_v, drive_v, out_v,
    small_sem, tile_sem, in_sem, w_sem, out_sem,
):
    segs, tracers, rows, points, total = dims
    pairs = rows // 2
    per = tracers * rows
    pair = 2 * points
    edges = (0, pairs - 1)
    fetches = [
        pltpu.make_async_copy(a, b, in_sem.at[i])
        for i, (a, b) in enumerate([(base_hbm, base), (dir_hbm, direction), (coup_hbm, coup)])
    ]
    for x in fetches:
        x.start()
    small, waits = start_fetches(edges, cols_ref, wet_ref, tiles_ref, cols, wet_v, tile_buf, small_sem, tile_sem)
    for x in fetches:
        x.wait()
    mix = mix_of(coup, cc)

    def native(ref, s, g):
        halves = [
            jnp.concatenate(
                [
                    ref[pl.ds(s * per + 2 * g + j, tracers, stride=rows), :],
                    jnp.zeros((PAD - tracers, points), jnp.float32),
                ],
                axis=0,
            )
            for j in range(2)
        ]
        return jnp.concatenate(halves, axis=1)

    units = [(s, g) for s in range(segs) for g in range(pairs)]
    slopes, starts = [], []
    for s, g in units:
        t = jnp.tanh(native(base, s, g))
        k = 1.0 - t * t
        slope_v[s, :, g * pair:(g + 1) * pair] = k
        slopes.append(k)
        starts.append(native(direction, s, g))
    drives = forced(mix, starts, slopes)
    for (s, g), d, k in zip(units, drives, slopes):
        drive_v[s, :, g * pair:(g + 1) * pair] = d
        if g in edges:
            high = k.astype(jnp.bfloat16)
            for i, x in enumerate((d, high)):
                for j in range(2):
                    at = 3 * points + (2 * i + j) * PAD
                    out_v[edges.index(g), s, at:at + PAD, :] = x[:, j * points:(j + 1) * points]
    for x in small:
        x.wait()
    outs = [
        pltpu.make_async_copy(slope_v, slope_ref, out_sem.at[0]),
        pltpu.make_async_copy(drive_v, drive_ref, out_sem.at[1]),
    ]
    for x in outs:
        x.start()

    def merged(i, s):
        for n, (c, j) in enumerate(BORDER[i]):
            c = c + i * 2 * REACH
            out_v[i, s, n * points:(n + 1) * points, :] = (
                w_v[s, i, c * points:(c + 1) * points, j * points:(j + 1) * points]
            )
        copy = pltpu.make_async_copy(w_v.at[s, i], w_ref.at[s, i], w_sem.at[s, i])
        copy.start()
        outs.append(copy)
        if s == segs - 1:
            copy = pltpu.make_async_copy(out_v.at[i], (left_ref, right_ref)[i], out_sem.at[2 + i])
            copy.start()
            outs.append(copy)

    merge_pairs(total, rows, edges, cols, wet_v, tile_buf, waits, (acc0, acc1), w_v, merged)
    for x in outs:
        x.wait()


def inner_kernel(
    dims, basis, cols_ref, wet_ref, tiles_ref, w_ref, gram_ref,
    cols, wet_v, tile_buf, acc0, acc1, small_sem, tile_sem,
):
    segs, tracers, rows, points, total = dims
    pairs = rows // 2
    kry = basis.shape[0]
    groups = tuple(range(1, pairs - 1))
    small, waits = start_fetches(groups, cols_ref, wet_ref, tiles_ref, cols, wet_v, tile_buf, small_sem, tile_sem)
    half = kry // 2 + 1

    def gram(i, acc):
        b = [basis[j, pl.ds(pl.multiple_of(i * rows, rows), rows), :] for j in range(kry)]
        return tuple(acc[m * kry + j] + b[j] * b[(j + m) % kry] for m in range(half) for j in range(kry))

    zero = jnp.zeros((rows, points), jnp.float32)
    sums = lax.fori_loop(0, segs * tracers, gram, (zero,) * (half * kry))
    for m in range(half):
        for j in range(kry):
            gram_ref[pl.ds(m * 8 + j, 1), :] = jnp.sum(sums[m * kry + j], axis=0, keepdims=True)
    for x in small:
        x.wait()
    merge_pairs(total, rows, groups, cols, wet_v, tile_buf, waits, (acc0, acc1), w_ref)


def steps_kernel(
    dims, slope, start, dir_ref, coup_ref, w_edge, w_inner, from_left, from_right, gram_in, basis, orth_ref, coef_ref,
    drive0, drive1, cc, follow, shalo, whalo, whalo2, hold, sent, came, part1, part2, gram1, gram2,
    send_sem, recv_sem, border_send, border_recv, follow_sem, red_sem1, red_sem2, gram_sem1, gram_sem2,
):
    segs, tracers, rows, points, kry, n_seg, n_blk, entries = dims
    pairs = rows // 2
    per = tracers * rows
    pair = 2 * points
    drive = (drive0, drive1)
    me_seg, me_blk = lax.axis_index("seg"), lax.axis_index("blk")
    left, right = lax.rem(me_blk + n_blk - 1, n_blk), lax.rem(me_blk + 1, n_blk)

    barrier = pltpu.get_barrier_semaphore()
    for i in range(1, n_blk):
        pl.semaphore_signal(barrier, inc=1, device_id={"blk": lax.rem(me_blk + i, n_blk)}, device_id_type=MESH)
    for i in range(1, n_seg):
        pl.semaphore_signal(barrier, inc=1, device_id={"seg": lax.rem(me_seg + i, n_seg)}, device_id_type=MESH)

    def lanes_of(g, count=1):
        return slice((g + 1) * pair, (g + 1 + count) * pair)

    mix = mix_of(coup_ref, cc)
    halos_in = (from_left, from_right)

    def force_into(units, to):
        values = forced(mix, [u for u, k, s, g in units], [k for u, k, s, g in units])
        for (u, k, s, g), v in zip(units, values):
            to[s, :, lanes_of(g)] = v

    def slope_of(s, g):
        return slope[s, :, g * pair:(g + 1) * pair]

    def beyond(s, side, i):
        at = 3 * points + 2 * i * PAD
        ref = halos_in[side]
        return jnp.concatenate([ref[s, at:at + PAD, :], ref[s, at + PAD:at + 2 * PAD, :]], axis=1)

    def slope_beyond(s, side):
        return shalo[side, s]

    edges = (0, pairs - 1)
    inner = range(1, pairs - 1)
    halo = (-1, pairs)
    for s in range(segs):
        drive0[s, :, pair:(pairs + 1) * pair] = start[s]
        for side in range(2):
            drive0[s, :, lanes_of(halo[side])] = beyond(s, side, 0)
            shalo[side, s] = beyond(s, side, 1).astype(jnp.float32)
            whalo[side, s] = jnp.zeros((pair, pair), jnp.bfloat16)
            for n, (c, j) in enumerate(BORDER[1 - side]):
                whalo[side, s, c * points:(c + 1) * points, j * points:(j + 1) * points] = (
                    halos_in[side][s, n * points:(n + 1) * points, :]
                )
    gram1[me_blk] = gram_in[...]
    follow_copy = pltpu.make_async_remote_copy(
        src_ref=dir_ref.at[0:per], dst_ref=follow, send_sem=follow_sem.at[0], recv_sem=follow_sem.at[1],
        device_id={"seg": lax.rem(me_seg + n_seg - 1, n_seg)}, device_id_type=MESH,
    )
    chunks = segs * tracers
    half = kry // 2 + 1

    def fold(a):
        return jnp.sum(a, axis=0, keepdims=True)

    def everyone(part, me, axis, count, sems):
        return [
            pltpu.make_async_remote_copy(
                src_ref=part.at[me], dst_ref=part.at[me],
                send_sem=sems.at[0, i - 1], recv_sem=sems.at[1, i - 1],
                device_id={axis: lax.rem(me + i, count)}, device_id_type=MESH,
            )
            for i in range(1, count)
        ]

    def total_of(part, copies, count):
        for x in copies:
            x.wait()
        result = part[0]
        for i in range(1, count):
            result = result + part[i]
        return result

    zero = jnp.zeros((rows, points), jnp.float32)
    gram_copies1 = everyone(gram1, me_blk, "blk", n_blk, gram_sem1)

    def message(n, side):
        return pltpu.make_async_remote_copy(
            src_ref=sent.at[n, side], dst_ref=came.at[n, 1 - side],
            send_sem=send_sem.at[n, side], recv_sem=recv_sem.at[n, 1 - side],
            device_id={"blk": (left, right)[side]}, device_id_type=MESH,
        )

    def arrival(n, side):
        return pltpu.make_async_remote_copy(
            src_ref=sent.at[n, 1 - side], dst_ref=came.at[n, side],
            send_sem=send_sem.at[n, 1 - side], recv_sem=recv_sem.at[n, side],
            device_id={"blk": (left, right)[1 - side]}, device_id_type=MESH,
        )

    def step(n, slot, halos, pieces):
        here, there = drive[slot], drive[1 - slot]
        own = [[None, None] for s in range(segs)]
        for s in range(segs):
            own[s][0] = dot(here[s, :, lanes_of(0, 2)], w_edge[s, 0, pair:3 * pair, :])
            own[s][1] = dot(here[s, :, lanes_of(pairs - 2, 2)], w_edge[s, 1, 0:2 * pair, :])
        def send():
            for side in range(2):
                for s in range(segs):
                    sent[n, side, s] = own[s][side].astype(jnp.bfloat16)
            if not halos:
                pl.semaphore_wait(barrier, n_blk + n_seg - 2)
            for side in range(2):
                message(n, side).start()
            for x in pieces:
                x.start()

        if halos:
            send()
        moved = {}
        for s in range(segs):
            for g in range(1, pairs - 1):
                moved[s, g] = dot(here[s, :, lanes_of(g - 1, 3)], w_inner[s, g - 1])
        if halos:
            mine = [
                [dot(there[s, :, lanes_of(edges[side])], whalo[side, s]) for side in range(2)]
                for s in range(segs)
            ]
        force_into([(moved[s, g], slope_of(s, g), s, g) for s in range(segs) for g in inner], there)
        if not halos:
            send()
        if halos:
            for side in range(2):
                arrival(n - 1, side).wait()
            force_into(
                [
                    (mine[s][side] + came[n - 1, side, s].astype(jnp.float32), slope_beyond(s, side), s, halo[side])
                    for s in range(segs)
                    for side in range(2)
                ],
                here,
            )
        for side in range(2):
            g = edges[side]
            for s in range(segs):
                moved[s, g] = own[s][side] + dot(
                    here[s, :, lanes_of(halo[side])], w_edge[s, side, side * 2 * pair:(side * 2 + 1) * pair, :]
                )
        force_into([(moved[s, g], slope_of(s, g), s, g) for s in range(segs) for g in edges], there)

    def beside(n, slot):
        here = drive[slot]
        for s in range(segs):
            r = (
                dot(here[s, :, lanes_of(1)], w_edge[s, 0, 2 * pair:3 * pair, :]),
                dot(here[s, :, lanes_of(pairs - 2)], w_edge[s, 1, 0:pair, :]),
            )
            for side in range(2):
                hold[slot, s, side] = r[side]
                sent[n, side, s] = r[side].astype(jnp.bfloat16)
        for side in range(2):
            message(n, side).start()

    def late_step(n, slot, finish):
        here, there = drive[slot], drive[1 - slot]
        moved = {}
        for s in range(segs):
            for g in inner:
                moved[s, g] = dot(here[s, :, lanes_of(g - 1, 3)], w_inner[s, g - 1])
        mine = {}
        for s in range(segs):
            for side in range(2):
                old = dot(there[s, :, lanes_of(halo[side])], whalo2[side, s])
                mine[s, side] = (
                    dot(there[s, :, lanes_of(edges[side])], whalo[side, s]) + jnp.where(n > SWITCH, old, 0.0)
                )
        if not finish:
            force_into([(moved[s, g], slope_of(s, g), s, g) for s in range(segs) for g in inner], there)
            beside(n + 1, 1 - slot)
        for side in range(2):
            arrival(n - 1, side).wait()
        force_into(
            [
                (mine[s, side] + came[n - 1, side, s].astype(jnp.float32), slope_beyond(s, side), s, halo[side])
                for s in range(segs)
                for side in range(2)
            ],
            here,
        )
        for side in range(2):
            g = edges[side]
            for s in range(segs):
                moved[s, g] = hold[slot, s, side] + dot(
                    here[s, :, lanes_of((-1, pairs - 1)[side], 2)], w_edge[s, side, side * pair:(side + 2) * pair, :]
                )
        if finish:
            for s in range(segs):
                for g in range(pairs):
                    for j in range(2):
                        orth_ref[pl.ds(s * per + 2 * g + j, tracers, stride=rows), :] = (
                            moved[s, g][:tracers, j * points:(j + 1) * points]
                        )
        else:
            force_into([(moved[s, g], slope_of(s, g), s, g) for s in range(segs) for g in edges], there)

    count = (SWITCH - 1) // segs
    size = pair // count
    borders = [
        [
            pltpu.make_async_remote_copy(
                src_ref=w_edge.at[s, side, pair + k * size:pair + (k + 1) * size, :],
                dst_ref=whalo2.at[1 - side, s, k * size:(k + 1) * size, :],
                send_sem=border_send.at[s * count + k, side], recv_sem=border_recv.at[s * count + k, side],
                device_id={"blk": (left, right)[side]}, device_id_type=MESH,
            )
            for side in range(2)
        ]
        for s in range(segs)
        for k in range(count)
    ]
    for n in range(SWITCH):
        step(n, n % 2, n > 0, borders[n] if n < len(borders) else [])
    follow_copy.start()
    for x in gram_copies1:
        x.start()
    beside(SWITCH, 1)
    for both in borders:
        for x in both:
            x.wait()

    def two_late(i, unused):
        late_step(SWITCH + 2 * i, 1, False)
        late_step(SWITCH + 2 * i + 1, 0, False)
        return unused

    lax.fori_loop(0, (STEPS - 1 - SWITCH) // 2, two_late, 0)
    late_step(STEPS - 1, 1, True)

    gram2[me_seg] = total_of(gram1, gram_copies1, n_blk)
    gram_copies2 = everyone(gram2, me_seg, "seg", n_seg, gram_sem2)
    for x in gram_copies2:
        x.start()
    follow_copy.wait()

    def project(i, acc):
        here = pl.ds(pl.multiple_of(i * rows, rows), rows)
        for s in range(segs):
            at = pl.ds(pl.multiple_of(i * rows, rows) + s * per, rows)
            if s < segs - 1:
                nxt = dir_ref[pl.ds(pl.multiple_of(i * rows, rows) + (s + 1) * per, rows), :]
            else:
                nxt = follow[here, :]
            shot = orth_ref[at, :] - nxt
            orth_ref[at, :] = shot
            acc = tuple(acc[j] + basis[j, at, :] * shot for j in range(kry)) + (acc[kry] + shot * shot,)
        return acc

    sums = lax.fori_loop(0, tracers, project, (zero,) * (kry + 1), unroll=4)
    for j in range(kry):
        part1[me_blk, pl.ds(j, 1), :] = fold(sums[j])
    part1[me_blk, pl.ds(8, 8), :] = sums[kry]

    copies = everyone(part1, me_blk, "blk", n_blk, red_sem1)
    for x in copies:
        x.start()
    for side in range(2):
        arrival(STEPS - 1, side).wait()
    part2[me_seg] = total_of(part1, copies, n_blk)
    copies = everyone(part2, me_seg, "seg", n_seg, red_sem2)
    for x in copies:
        x.start()
    gramd = jnp.sum(total_of(gram2, gram_copies2, n_seg), axis=1, keepdims=True)
    sumd = jnp.sum(total_of(part2, copies, n_seg), axis=1, keepdims=True)
    h = sumd[0:kry]
    hv = [sumd[j:j + 1] for j in range(kry)]
    quad = jnp.zeros((kry, 1), jnp.float32)
    for m in range(half):
        turned = h if m == 0 else jnp.concatenate([h[m:], h[:m]], axis=0)
        weight = 1.0 if m == 0 or 2 * m == kry else 2.0
        quad = quad + weight * (turned * gramd[m * 8:m * 8 + kry])
    quad = h * (quad - 2.0 * h) + sumd[8:16]
    square = jnp.sum(jnp.broadcast_to(quad, (kry, points)), axis=0, keepdims=True)
    length = jnp.sqrt(jnp.maximum(square, 0.0) / entries)
    coef_ref[kry] = length[0, 0]
    for j in range(kry):
        coef_ref[j] = hv[j][0, 0]
    wide = [jnp.broadcast_to(x, (rows, points)) for x in hv]

    def subtract(i, unused):
        at = pl.ds(pl.multiple_of(i * rows, rows), rows)
        a = hv_sum([wide[j] * basis[j, at, :] for j in range(kry)])
        orth_ref[at, :] = orth_ref[at, :] - a
        return unused

    lax.fori_loop(0, chunks, subtract, 0, unroll=8)


def hv_sum(terms):
    while len(terms) > 1:
        terms = [sum(terms[i:i + 2]) for i in range(0, len(terms), 2)]
    return terms[0]


def on_device(n_seg, n_blk, base_state, direction, coupling, tiles, columns, wet, basis):
    segs, tracers, rows, points = direction.shape
    stored = tiles.shape[2]
    kry = basis.shape[0]
    total = rows * n_blk
    entries = float(segs * n_seg * tracers * total * points)
    pairs = rows // 2
    pair = 2 * points
    wide = 2 * REACH + 2
    flat = segs * tracers * rows
    base_flat = base_state.reshape(flat, points)
    dir_flat = direction.reshape(flat, points)
    basis_flat = basis.reshape(kry, flat, points)
    in_vmem = pl.BlockSpec(memory_space=pltpu.VMEM)
    in_hbm = pl.BlockSpec(memory_space=pltpu.HBM)
    bf16, f32 = jnp.bfloat16, jnp.float32
    shape = jax.ShapeDtypeStruct

    def scratch_of(count):
        return [
            pltpu.SMEM((segs, rows, stored), jnp.int32),
            pltpu.VMEM((rows, points), jnp.int32),
            pltpu.VMEM((segs, 2 * count, stored, points, points), bf16),
            pltpu.VMEM((2 * REACH + 1, points, points), f32),
            pltpu.VMEM((2 * REACH + 1, points, points), f32),
        ]

    def sems_of(count):
        return [pltpu.SemaphoreType.DMA((2,)), pltpu.SemaphoreType.DMA((segs, 2 * count))]

    dims = (segs, tracers, rows, points, total)
    work = segs * rows * stored * points * points
    border = shape((segs, 3 * points + 4 * PAD, points), bf16)
    w_edge, slope, start, to_left, to_right = pl.pallas_call(
        functools.partial(edge_kernel, dims),
        out_shape=(
            shape((segs, 2, wide * points, pair), bf16), shape((segs, PAD, rows * points), f32),
            shape((segs, PAD, rows * points), bf16), border, border,
        ),
        in_specs=[in_hbm] * 6,
        out_specs=(in_hbm,) * 5,
        scratch_shapes=scratch_of(2) + [
            pltpu.VMEM((PAD, 2 * PAD), f32),
            pltpu.VMEM((flat, points), f32),
            pltpu.VMEM((flat, points), f32),
            pltpu.VMEM((tracers, tracers), f32),
            pltpu.VMEM((segs, 2, wide * points, pair), bf16),
            pltpu.VMEM((segs, PAD, rows * points), f32),
            pltpu.VMEM((segs, PAD, rows * points), bf16),
            pltpu.VMEM((2, segs, 3 * points + 4 * PAD, points), bf16),
        ] + sems_of(2) + [
            pltpu.SemaphoreType.DMA((3,)),
            pltpu.SemaphoreType.DMA((segs, 2)),
            pltpu.SemaphoreType.DMA((4,)),
        ],
        compiler_params=pltpu.CompilerParams(vmem_limit_bytes=56 << 20),
        cost_estimate=pl.CostEstimate(flops=8 * work, bytes_accessed=work, transcendentals=0),
        name="edge",
    )(base_flat, dir_flat, coupling, columns, wet, tiles)
    ring = range(n_blk)
    from_right = lax.ppermute(to_left, "blk", [(i, (i + n_blk - 1) % n_blk) for i in ring])
    from_left = lax.ppermute(to_right, "blk", [(i, (i + 1) % n_blk) for i in ring])
    w_inner, gram = pl.pallas_call(
        functools.partial(inner_kernel, dims),
        out_shape=(
            shape((segs, pairs - 2, wide * points, pair), bf16), shape(((kry // 2 + 1) * 8, points), f32),
        ),
        in_specs=[in_vmem] + [in_hbm] * 3,
        out_specs=(in_vmem,) * 2,
        scratch_shapes=scratch_of(pairs - 2) + sems_of(pairs - 2),
        compiler_params=pltpu.CompilerParams(vmem_limit_bytes=48 << 20),
        cost_estimate=pl.CostEstimate(flops=8 * work, bytes_accessed=work, transcendentals=0),
        name="inner",
    )(basis_flat, columns, wet, tiles)
    dims = (segs, tracers, rows, points, kry, n_seg, n_blk, entries)
    half = (kry // 2 + 1) * 8
    orth, coef = pl.pallas_call(
        functools.partial(steps_kernel, dims),
        out_shape=(
            jax.ShapeDtypeStruct((flat, points), jnp.float32),
            jax.ShapeDtypeStruct((kry + 1,), jnp.float32),
        ),
        in_specs=[in_vmem] * 10,
        out_specs=(in_vmem, pl.BlockSpec(memory_space=pltpu.SMEM)),
        scratch_shapes=[
            pltpu.VMEM((segs, PAD, (pairs + 2) * pair), jnp.bfloat16),
            pltpu.VMEM((segs, PAD, (pairs + 2) * pair), jnp.bfloat16),
            pltpu.VMEM((PAD, 2 * PAD), jnp.float32),
            pltpu.VMEM((tracers * rows, points), jnp.float32),
            pltpu.VMEM((2, segs, PAD, pair), jnp.float32),
            pltpu.VMEM((2, segs, pair, pair), jnp.bfloat16),
            pltpu.VMEM((2, segs, pair, pair), jnp.bfloat16),
            pltpu.VMEM((2, segs, 2, PAD, pair), jnp.float32),
            pltpu.VMEM((STEPS, 2, segs, PAD, pair), jnp.bfloat16),
            pltpu.VMEM((STEPS, 2, segs, PAD, pair), jnp.bfloat16),
            pltpu.VMEM((n_blk, 16, points), jnp.float32),
            pltpu.VMEM((n_seg, 16, points), jnp.float32),
            pltpu.VMEM((n_blk, half, points), jnp.float32),
            pltpu.VMEM((n_seg, half, points), jnp.float32),
            pltpu.SemaphoreType.DMA((STEPS, 2)),
            pltpu.SemaphoreType.DMA((STEPS, 2)),
            pltpu.SemaphoreType.DMA((SWITCH - 1, 2)),
            pltpu.SemaphoreType.DMA((SWITCH - 1, 2)),
            pltpu.SemaphoreType.DMA((2,)),
            pltpu.SemaphoreType.DMA((2, n_blk - 1)),
            pltpu.SemaphoreType.DMA((2, n_seg - 1)),
            pltpu.SemaphoreType.DMA((2, n_blk - 1)),
            pltpu.SemaphoreType.DMA((2, n_seg - 1)),
        ],
        compiler_params=pltpu.CompilerParams(
            collective_id=0, has_side_effects=True, vmem_limit_bytes=40 << 20
        ),
        name="steps",
    )(slope, start, dir_flat, coupling, w_edge, w_inner, from_left, from_right, gram, basis_flat)
    return orth.reshape(direction.shape), coef


def solution(mesh):
    in_specs = (
        P(("groups", "seg"), None, "blk", None),
        P(("groups", "seg"), None, "blk", None),
        P("groups", None),
        P("seg", "blk", None, None, None),
        P("seg", "blk", None),
        P("blk", None),
        P(None, ("groups", "seg"), None, "blk", None),
    )
    out_specs = (P(("groups", "seg"), None, "blk", None), P("groups"))
    body = functools.partial(on_device, mesh.shape["seg"], mesh.shape["blk"])
    return jax.shard_map(body, mesh=mesh, in_specs=in_specs, out_specs=out_specs, check_vma=False)
```
